256 devices in a mesh: seq: 32 (over z, x), grp: 8 (over y, core).
Axes of the slice: x: 4, y: 4, z: 8, core: 2. Of those that a mesh axis runs over, the one named last changes fastest.
Arguments:
- queries: bfloat16 [8, 4096, 2048], P('grp', 'seq'), may hold values from -500 to 500
- grad_out: bfloat16 [8, 4096, 2048], P('grp', 'seq'), may hold values from -6 to 6
- enc_states: bfloat16 [8, 256, 128, 512], P('grp', 'seq'), may hold values from -6 to 6
- neighbour_ids: int32 [8, 64, 2], P('grp', 'seq'), may hold values from 0 to 255, as said below
- kv_weight: bfloat16 [2, 512, 2048], replicated, may hold values from -0.25 to 0.25
Outputs:
- grad_queries: bfloat16 [8, 4096, 2048], P('grp', 'seq')
- grad_states: bfloat16 [8, 256, 128, 512], P('grp', 'seq')
- grad_weight: float32 [2, 512, 2048], P(None, 'seq', 'grp')
The draws below stay inside these ranges and needn't reach their ends.
Inputs may be any that keep to these rules, and one draw needn't show every extreme that they name: `neighbour_ids`: block b is held at position b % 8 by the device of index b // 8 along seq. Of the 4 references of one device's spans, at most 1 name blocks held by any one device, and that many do so for some device.
All inputs are finite; a program needn't handle non-finite values.
Results may differ from the reference program's by a relative error of at most 0.012.
The reference program's roundings to bfloat16 on the way (of `states`, `weights_b`, `grad_v`, `grad_s`, `grad_k` and `grad_e`) count: a program that leaves them out, or rounds other values in their place, can miss the bound.
Values may be sent and summed in bfloat16 or wider, within the bound.
A program may use at most 128 MiB of HBM per device.

```python
import math
import jax
import jax.numpy as jnp
from jax import lax

H = 16
DH = 128
ENC = 512
SPAN = 64
NBR = 2
NLEN = 128
NB_DEV = 8
HD = 2048
TOKENS = 4096
SPANS = 64
REFS = 4
NBLK = 256
N_SEQ = 32
N_GRP = 8


def draw_queries(key, part):
    key = jax.random.fold_in(key, 11)
    shape = (N_GRP, TOKENS, HD)
    base = jax.random.normal(key, shape, jnp.float32)
    return base.astype(jnp.bfloat16)


def draw_grad_out(key, part):
    key = jax.random.fold_in(key, 17)
    shape = (N_GRP, TOKENS, HD)
    base = jnp.clip(jax.random.normal(key, shape, jnp.float32), -6.0, 6.0)
    return base.astype(jnp.bfloat16)


def draw_neighbour_ids(key, part):
    key = jax.random.fold_in(key, 5)
    first_key, second_key = jax.random.split(key)
    device_keys = jax.random.split(first_key, N_GRP * N_SEQ)
    orders = jax.vmap(lambda one_key: jax.random.permutation(one_key, N_SEQ))(device_keys)
    columns = jnp.arange(REFS) % N_SEQ
    owners = orders[:, columns]
    local_slot = jax.random.randint(second_key, (N_GRP * N_SEQ, REFS), 0, NB_DEV)
    block_ids = owners * NB_DEV + local_slot
    return block_ids.reshape(N_GRP, SPANS, NBR).astype(jnp.int32)


def steps_of(rng, extent, cuts, smallest, top_value):
    def one(axis_at, parts):
        steps = jax.random.uniform(jax.random.fold_in(jax.random.fold_in(rng, 6), axis_at), (parts,), jnp.float32, smallest / len(cuts), top_value / len(cuts))
        return jnp.repeat(jnp.exp(steps), extent[axis_at] // parts).reshape((-1,) + (1,) * (len(extent) - axis_at - 1))

    gain = one(*cuts[0])
    for cut in cuts[1:]:
        gain = gain * one(*cut)
    return gain


def scatter_about(key, extent, width, most, pieces=(), held_as=jnp.bfloat16):
    level = steps_of(key, extent, pieces, -0.22, 0.18) if pieces else 1.0
    values = jax.random.normal(key, extent, jnp.float32) * width * level
    return jnp.minimum(jnp.maximum(values, -most), most).astype(held_as)


def setup_inputs(seed: int = 0) -> dict:
    streams_of = jax.random.split(jax.random.key(seed), 6)
    return {
        "queries": draw_queries(jax.random.fold_in(streams_of[5], 71), 0),
        "grad_out": draw_grad_out(jax.random.fold_in(streams_of[5], 71), 0),
        "enc_states": scatter_about(streams_of[2], (N_GRP, NBLK, NLEN, ENC), 1.0, 6.0, ((0, 8), (1, 32))),
        "neighbour_ids": draw_neighbour_ids(jax.random.fold_in(streams_of[5], 71), 0),
        "kv_weight": scatter_about(streams_of[4], (2, ENC, HD), ENC ** -0.5, 0.25),
    }


def rounded(values_f):
    return lax.optimization_barrier(values_f.astype(jnp.bfloat16))

def span_grads(query, grad_o, states, kv_weight):
    score_scale = 1.0 / math.sqrt(DH)
    flat_states = states.reshape(NBR * NLEN, ENC)
    key_rows = rounded(jnp.dot(flat_states, kv_weight[0], preferred_element_type=jnp.float32))
    value_rows = rounded(jnp.dot(flat_states, kv_weight[1], preferred_element_type=jnp.float32))
    query_h = query.reshape(SPAN, H, DH).astype(jnp.float32)
    key_h = key_rows.reshape(NBR * NLEN, H, DH).astype(jnp.float32)
    value_h = value_rows.reshape(NBR * NLEN, H, DH).astype(jnp.float32)
    grad_h = grad_o.reshape(SPAN, H, DH).astype(jnp.float32)
    scores = jnp.einsum('qhd,khd->hqk', query_h, key_h) * score_scale
    top_score = lax.optimization_barrier(jnp.max(scores, axis=-1, keepdims=True))
    expo = jnp.exp(scores - top_score)
    weights_f = expo / lax.optimization_barrier(jnp.sum(expo, axis=-1, keepdims=True))
    weights_b = rounded(weights_f).astype(jnp.float32)
    attended = jnp.einsum('hqk,khd->qhd', weights_b, value_h)
    row_delta = lax.optimization_barrier(jnp.sum(grad_h * attended, axis=-1))
    grad_v = jnp.einsum('hqk,qhd->khd', weights_b, grad_h).astype(jnp.bfloat16)
    grad_p = jnp.einsum('qhd,khd->hqk', grad_h, value_h)
    grad_s = rounded(weights_f * (grad_p - jnp.transpose(row_delta)[:, :, None]) * score_scale).astype(jnp.float32)
    grad_q = jnp.einsum('hqk,khd->qhd', grad_s, key_h).astype(jnp.bfloat16)
    grad_k = jnp.einsum('hqk,qhd->khd', grad_s, query_h).astype(jnp.bfloat16)
    flat_k = grad_k.reshape(NBR * NLEN, HD)
    flat_v = grad_v.reshape(NBR * NLEN, HD)
    grad_e = jnp.dot(flat_k, kv_weight[0].T, preferred_element_type=jnp.float32)
    grad_e = (grad_e + jnp.dot(flat_v, kv_weight[1].T, preferred_element_type=jnp.float32)).astype(jnp.bfloat16)
    weight_part = jnp.stack([jnp.dot(flat_states.T, flat_k, preferred_element_type=jnp.float32), jnp.dot(flat_states.T, flat_v, preferred_element_type=jnp.float32)])
    return (grad_q.reshape(SPAN, HD), grad_e.reshape(NBR, NLEN, ENC), weight_part)

def reference(queries, grad_out, enc_states, neighbour_ids, kv_weight):

    def group_step(weight_total, group_data):
        group_query, group_grad, group_states, group_ids = group_data

        def span_step(running, span_item):
            state_total, weight_acc = running
            query, grad_o, nbr_pair = span_item
            states = jnp.take(group_states, nbr_pair.astype(jnp.int32), axis=0)
            grad_q, grad_e, weight_part = span_grads(query, grad_o, states, kv_weight)
            state_total = state_total.at[nbr_pair.astype(jnp.int32)].add(grad_e.astype(jnp.float32))
            return ((state_total, weight_acc + weight_part), grad_q)
        start_state = (jnp.zeros((NBLK, NLEN, ENC), jnp.float32), weight_total)
        span_data = (group_query.reshape(SPANS, SPAN, HD), group_grad.reshape(SPANS, SPAN, HD), group_ids)
        (state_total, weight_total), grad_rows = lax.scan(span_step, start_state, span_data)
        return (weight_total, (grad_rows.reshape(TOKENS, HD), state_total.astype(jnp.bfloat16)))
    weight_zero = jnp.zeros((2, ENC, HD), jnp.float32)
    weight_total, (grad_queries, grad_states) = lax.scan(group_step, weight_zero, (queries, grad_out, enc_states, neighbour_ids))
    return (grad_queries, grad_states, weight_total)
```

```python
import functools
import math

import jax
import jax.numpy as jnp
from jax import lax
from jax.experimental import pallas as pl
from jax.experimental.pallas import tpu as pltpu
from jax.sharding import PartitionSpec as P

DH = 128
BF = jnp.bfloat16
F32 = jnp.float32
MESH = pl.DeviceIdType.MESH
NT = (((1,), (1,)), ((), ()))
TN = (((0,), (0,)), ((), ()))


def attention_kernel(states_ref, w_ref, q_ref, go_ref, gq_ref, ge_ref, dw_ref, st_ref, acc_ref):
    step = pl.program_id(0)
    scale = 1.0 / math.sqrt(DH)

    @pl.when(step == 0)
    def _():
        st_ref[...] = states_ref[...].T
        acc_ref[...] = jnp.zeros_like(acc_ref)

    states = states_ref[...]
    wk = w_ref[0]
    wv = w_ref[1]
    keys = jnp.dot(states, wk, preferred_element_type=F32).astype(BF)
    values = jnp.dot(states, wv, preferred_element_type=F32).astype(BF)
    blank = jnp.zeros((64, DH), BF)
    gk_parts = []
    gv_parts = []
    for span in range(2):
        q = q_ref[span * 64 : span * 64 + 64, :]
        go = go_ref[span * 64 : span * 64 + 64, :]
        key = keys[span * 256 : span * 256 + 256, :]
        value = values[span * 256 : span * 256 + 256, :]
        qd = jnp.concatenate(
            [
                jnp.concatenate([q[:, :DH], blank], axis=1),
                jnp.concatenate([blank, q[:, DH:]], axis=1),
            ],
            axis=0,
        )
        gd = jnp.concatenate(
            [
                jnp.concatenate([go[:, :DH], blank], axis=1),
                jnp.concatenate([blank, go[:, DH:]], axis=1),
            ],
            axis=0,
        )
        scores = lax.dot_general(key, qd, NT, preferred_element_type=F32) * scale
        top = jnp.max(scores, axis=0, keepdims=True)
        expo = jnp.exp(scores - top)
        weights = expo / jnp.sum(expo, axis=0, keepdims=True)
        weights_b = weights.astype(BF)
        gp = lax.dot_general(value, gd, NT, preferred_element_type=F32)
        delta = jnp.sum(weights_b.astype(F32) * gp, axis=0, keepdims=True)
        gs = (weights * (gp - delta) * scale).astype(BF)
        gv_parts.append(jnp.dot(weights_b, gd, preferred_element_type=F32).astype(BF))
        gk_parts.append(jnp.dot(gs, qd, preferred_element_type=F32).astype(BF))
        gq = lax.dot_general(gs, key, TN, preferred_element_type=F32).astype(BF)
        gq_ref[span * 64 : span * 64 + 64, :DH] = gq[:64, :DH]
        gq_ref[span * 64 : span * 64 + 64, DH:] = gq[64:, DH:]
    gk = jnp.concatenate(gk_parts, axis=0)
    gv = jnp.concatenate(gv_parts, axis=0)
    total = acc_ref[...]
    total = total + lax.dot_general(gk, wk, NT, preferred_element_type=F32)
    total = total + lax.dot_general(gv, wv, NT, preferred_element_type=F32)
    acc_ref[...] = total

    @pl.when(step == pl.num_programs(0) - 1)
    def _():
        ge_ref[...] = total.astype(BF)

    turned = st_ref[...]
    for kind, part in enumerate((gk, gv)):
        share = jnp.dot(turned, part, preferred_element_type=F32).astype(BF)
        for z in range(8):
            for x in range(4):
                row = (z * 4 + x) * 16
                dw_ref[0, x, kind, z] = share[row : row + 16, :]


def attention(states, weights, queries, grad_out):
    keys, enc = states.shape
    tokens, width = queries.shape
    return pl.pallas_call(
        attention_kernel,
        grid=(8,),
        in_specs=[
            pl.BlockSpec((keys, enc), lambda i: (0, 0)),
            pl.BlockSpec((2, enc, 256), lambda i: (0, 0, i)),
            pl.BlockSpec((tokens, 256), lambda i: (0, i)),
            pl.BlockSpec((tokens, 256), lambda i: (0, i)),
        ],
        out_specs=[
            pl.BlockSpec((tokens, 256), lambda i: (0, i)),
            pl.BlockSpec((keys, enc), lambda i: (0, 0)),
            pl.BlockSpec((1, 4, 2, 8, 16, 256), lambda i: (i, 0, 0, 0, 0, 0)),
        ],
        out_shape=[
            jax.ShapeDtypeStruct((tokens, width), BF),
            jax.ShapeDtypeStruct((keys, enc), BF),
            jax.ShapeDtypeStruct((8, 4, 2, 8, 16, 256), BF),
        ],
        scratch_shapes=[pltpu.VMEM((enc, keys), BF), pltpu.VMEM((keys, enc), F32)],
        compiler_params=pltpu.CompilerParams(vmem_limit_bytes=40 * 2**20),
        cost_estimate=pl.CostEstimate(
            flops=7_200_000_000, bytes_accessed=12_000_000, transcendentals=600_000
        ),
    )(states, weights, queries, grad_out)


def reduce_kernel(
    dw_ref, out_ref, pair_in, held, y_half, y_in, x_half, x_in, z_in, core_sem, y_sem, x_sem, z_sem
):
    seq = lax.axis_index("seq")
    grp = lax.axis_index("grp")
    z = seq // 4
    x = seq % 4
    y = grp // 2
    core = grp % 2

    def at(zz, xx, yy, cc):
        return {
            "seq": (zz + 8) % 8 * 4 + (xx + 4) % 4,
            "grp": (yy + 4) % 4 * 2 + cc,
        }

    barrier = pltpu.get_barrier_semaphore()
    friends = [at(z, x, y, 1 - core)]
    friends += [at(z, x, y + step, core) for step in (1, 3)]
    friends += [at(z, x + step, y, core) for step in (1, 3)]
    friends += [at(z + step, x, y, core) for step in range(1, 8)]
    for friend in friends:
        pl.semaphore_signal(barrier, inc=1, device_id=friend, device_id_type=MESH)
    pl.semaphore_wait(barrier, len(friends))

    def send(src, dst, sems, slot, target):
        copy = pltpu.make_async_remote_copy(
            src_ref=src,
            dst_ref=dst,
            send_sem=sems.at[0, slot],
            recv_sem=sems.at[1, slot],
            device_id=target,
            device_id_type=MESH,
        )
        copy.start()
        return copy

    offsets = (2, 1, 3, 0)
    swaps = []
    for slot, offset in enumerate(offsets):
        theirs = (y + offset) % 4 * 2 + 1 - core
        swaps.append(
            send(dw_ref.at[theirs], pair_in.at[slot], core_sem, slot, at(z, x, y, 1 - core))
        )

    def add_pair(slot, offset):
        swaps[slot].wait_recv()
        mine = (y + offset) % 4 * 2 + core
        for part in range(4):
            held[slot, part] = (
                dw_ref[mine, part].astype(F32) + pair_in[slot, part].astype(F32)
            ).astype(BF)

    add_pair(0, 2)
    up = send(held.at[0, pl.ds(0, 2)], y_half.at[0], y_sem, 0, at(z, x, y + 1, core))
    down = send(held.at[0, pl.ds(2, 2)], y_half.at[1], y_sem, 1, at(z, x, y - 1, core))
    add_pair(1, 1)
    add_pair(2, 3)
    add_pair(3, 0)
    up.wait_recv()
    for part in range(2):
        held[1, part] = (held[1, part].astype(F32) + y_half[0, part].astype(F32)).astype(BF)
    up2 = send(held.at[1], y_in.at[0], y_sem, 2, at(z, x, y + 1, core))
    down.wait_recv()
    for part in range(2):
        held[2, part + 2] = (
            held[2, part + 2].astype(F32) + y_half[1, part].astype(F32)
        ).astype(BF)
    down2 = send(held.at[2], y_in.at[1], y_sem, 3, at(z, x, y - 1, core))
    up2.wait_recv()
    down2.wait_recv()

    def y_total(offset):
        part = (x + offset) % 4
        return (
            held[3, part].astype(F32)
            + y_in[0, part].astype(F32)
            + y_in[1, part].astype(F32)
        )

    held[4, 0] = y_total(2).astype(BF)
    xup = send(held.at[4, 0, 0], x_half.at[0], x_sem, 0, at(z, x + 1, y, core))
    xdown = send(held.at[4, 0, 1], x_half.at[1], x_sem, 1, at(z, x - 1, y, core))
    ahead = y_total(1)
    behind = y_total(3)
    own = y_total(0)
    xup.wait_recv()
    held[4, 1, 0] = (ahead[0] + x_half[0].astype(F32)).astype(BF)
    held[4, 1, 1] = ahead[1].astype(BF)
    xup2 = send(held.at[4, 1], x_in.at[0], x_sem, 2, at(z, x + 1, y, core))
    xdown.wait_recv()
    held[4, 2, 0] = behind[0].astype(BF)
    held[4, 2, 1] = (behind[1] + x_half[1].astype(F32)).astype(BF)
    xdown2 = send(held.at[4, 2], x_in.at[1], x_sem, 3, at(z, x - 1, y, core))
    xup2.wait_recv()
    xdown2.wait_recv()
    held[4, 3] = (own + x_in[0].astype(F32) + x_in[1].astype(F32)).astype(BF)

    zs = []
    for step in (4, 3, 5, 2, 6, 1, 7):
        target = (z + step) % 8
        zs.append(
            send(
                held.at[4, 3, :, target], z_in.at[step - 1], z_sem, step - 1, at(z + step, x, y, core)
            )
        )
    result = held[4, 3, :, z].astype(F32)
    for copy, step in zip(zs, (4, 3, 5, 2, 6, 1, 7)):
        copy.wait_recv()
        result = result + z_in[step - 1].astype(F32)
    out_ref[...] = result
    for copy in swaps + [up, down, up2, down2, xup, xdown, xup2, xdown2] + zs:
        copy.wait_send()


def reduce_weights(dw):
    return pl.pallas_call(
        reduce_kernel,
        in_specs=[pl.BlockSpec(memory_space=pltpu.VMEM)],
        out_specs=pl.BlockSpec(memory_space=pltpu.VMEM),
        out_shape=jax.ShapeDtypeStruct((2, 16, 256), F32),
        scratch_shapes=[
            pltpu.VMEM((4, 4, 2, 8, 16, 256), BF),
            pltpu.VMEM((5, 4, 2, 8, 16, 256), BF),
            pltpu.VMEM((2, 2, 2, 8, 16, 256), BF),
            pltpu.VMEM((2, 4, 2, 8, 16, 256), BF),
            pltpu.VMEM((2, 8, 16, 256), BF),
            pltpu.VMEM((2, 2, 8, 16, 256), BF),
            pltpu.VMEM((7, 2, 16, 256), BF),
            pltpu.SemaphoreType.DMA((2, 4)),
            pltpu.SemaphoreType.DMA((2, 4)),
            pltpu.SemaphoreType.DMA((2, 4)),
            pltpu.SemaphoreType.DMA((2, 7)),
        ],
        compiler_params=pltpu.CompilerParams(
            collective_id=1, has_side_effects=True, vmem_limit_bytes=40 * 2**20
        ),
    )(dw)


def body(queries, grad_out, enc_states, neighbour_ids, kv_weight):
    seq_count = lax.axis_size("seq")
    blocks_dev = enc_states.shape[1]
    nbr_len = enc_states.shape[2]
    enc_width = enc_states.shape[3]
    flat_refs = neighbour_ids.reshape(-1)
    ref_count = flat_refs.shape[0]
    owners = flat_refs // blocks_dev
    local_slot = flat_refs % blocks_dev
    placing = owners[:, None] == jnp.arange(seq_count)[None, :]
    wanted = jnp.sum(jnp.where(placing, local_slot[:, None] + 1, 0), axis=0) - 1
    asked = lax.all_to_all(
        wanted.reshape(seq_count, 1), "seq", split_axis=0, concat_axis=0, tiled=True
    ).reshape(-1)
    replies = jnp.take(enc_states[0], jnp.maximum(asked, 0), axis=0)
    arrived = lax.all_to_all(replies, "seq", split_axis=0, concat_axis=0, tiled=True)
    states = jnp.take(arrived, owners, axis=0)
    flat_states = states.reshape(ref_count * nbr_len, enc_width)
    gq, grad_e, dw = attention(flat_states, kv_weight, queries[0], grad_out[0])
    grad_weight = reduce_weights(dw)
    placing_b = placing.astype(BF)
    grad_e = grad_e.reshape(ref_count, nbr_len, enc_width)
    sending = jnp.einsum("rs,rtc->stc", placing_b, grad_e, preferred_element_type=F32).astype(BF)
    picking = (asked[:, None] == jnp.arange(blocks_dev)[None, :]).astype(BF)
    summed = jnp.einsum(
        "sb,stc->btc",
        picking,
        lax.all_to_all(sending, "seq", split_axis=0, concat_axis=0, tiled=True),
        preferred_element_type=F32,
    )
    grad_states = summed.astype(BF)[None]
    return (gq[None], grad_states, grad_weight)


def solution(mesh):
    placed = (
        P("grp", "seq", None),
        P("grp", "seq", None),
        P("grp", "seq", None, None),
        P("grp", "seq", None),
        P(),
    )
    return jax.shard_map(
        body,
        mesh=mesh,
        in_specs=placed,
        out_specs=(P("grp", "seq", None), P("grp", "seq", None, None), P(None, "seq", "grp")),
        check_vma=False,
    )
```

```python
import functools
import math

import jax
import jax.numpy as jnp
from jax import lax
from jax.experimental import pallas as pl
from jax.experimental.pallas import tpu as pltpu
from jax.sharding import PartitionSpec as P

DH = 128
BF = jnp.bfloat16
F32 = jnp.float32
MESH = pl.DeviceIdType.MESH
NT = (((1,), (1,)), ((), ()))
TN = (((0,), (0,)), ((), ()))


def attention_kernel(states_ref, w_ref, q_ref, go_ref, gq_ref, ge_ref, dw_ref, st_ref, acc_ref):
    step = pl.program_id(0)
    scale = 1.0 / math.sqrt(DH)

    @pl.when(step == 0)
    def _():
        st_ref[...] = states_ref[...].T
        acc_ref[...] = jnp.zeros_like(acc_ref)

    states = states_ref[...]
    wk = w_ref[0]
    wv = w_ref[1]
    keys = jnp.dot(states, wk, preferred_element_type=F32).astype(BF)
    values = jnp.dot(states, wv, preferred_element_type=F32).astype(BF)
    blank = jnp.zeros((64, DH), BF)
    gk_parts = []
    gv_parts = []
    for span in range(2):
        q = q_ref[span * 64 : span * 64 + 64, :]
        go = go_ref[span * 64 : span * 64 + 64, :]
        key = keys[span * 256 : span * 256 + 256, :]
        value = values[span * 256 : span * 256 + 256, :]
        qd = jnp.concatenate(
            [
                jnp.concatenate([q[:, :DH], blank], axis=1),
                jnp.concatenate([blank, q[:, DH:]], axis=1),
            ],
            axis=0,
        )
        gd = jnp.concatenate(
            [
                jnp.concatenate([go[:, :DH], blank], axis=1),
                jnp.concatenate([blank, go[:, DH:]], axis=1),
            ],
            axis=0,
        )
        scores = lax.dot_general(key, qd, NT, preferred_element_type=F32) * scale
        top = jnp.max(scores, axis=0, keepdims=True)
        expo = jnp.exp(scores - top)
        weights = expo / jnp.sum(expo, axis=0, keepdims=True)
        weights_b = weights.astype(BF)
        gp = lax.dot_general(value, gd, NT, preferred_element_type=F32)
        delta = jnp.sum(weights_b.astype(F32) * gp, axis=0, keepdims=True)
        gs = (weights * (gp - delta) * scale).astype(BF)
        gv_parts.append(jnp.dot(weights_b, gd, preferred_element_type=F32).astype(BF))
        gk_parts.append(jnp.dot(gs, qd, preferred_element_type=F32).astype(BF))
        gq = lax.dot_general(gs, key, TN, preferred_element_type=F32).astype(BF)
        gq_ref[span * 64 : span * 64 + 64, :DH] = gq[:64, :DH]
        gq_ref[span * 64 : span * 64 + 64, DH:] = gq[64:, DH:]
    gk = jnp.concatenate(gk_parts, axis=0)
    gv = jnp.concatenate(gv_parts, axis=0)
    total = acc_ref[...]
    total = total + lax.dot_general(gk, wk, NT, preferred_element_type=F32)
    total = total + lax.dot_general(gv, wv, NT, preferred_element_type=F32)
    acc_ref[...] = total

    @pl.when(step == pl.num_programs(0) - 1)
    def _():
        ge_ref[...] = total.astype(BF)

    turned = st_ref[...]
    for kind, part in enumerate((gk, gv)):
        share = jnp.dot(turned, part, preferred_element_type=F32).astype(BF)
        for z in range(8):
            for x in range(4):
                row = (z * 4 + x) * 16
                dw_ref[0, x, kind, z] = share[row : row + 16, :]


def attention(states, weights, queries, grad_out):
    keys, enc = states.shape
    tokens, width = queries.shape
    return pl.pallas_call(
        attention_kernel,
        grid=(8,),
        in_specs=[
            pl.BlockSpec((keys, enc), lambda i: (0, 0)),
            pl.BlockSpec((2, enc, 256), lambda i: (0, 0, i)),
            pl.BlockSpec((tokens, 256), lambda i: (0, i)),
            pl.BlockSpec((tokens, 256), lambda i: (0, i)),
        ],
        out_specs=[
            pl.BlockSpec((tokens, 256), lambda i: (0, i)),
            pl.BlockSpec((keys, enc), lambda i: (0, 0)),
            pl.BlockSpec((1, 4, 2, 8, 16, 256), lambda i: (i, 0, 0, 0, 0, 0)),
        ],
        out_shape=[
            jax.ShapeDtypeStruct((tokens, width), BF),
            jax.ShapeDtypeStruct((keys, enc), BF),
            jax.ShapeDtypeStruct((8, 4, 2, 8, 16, 256), BF),
        ],
        scratch_shapes=[pltpu.VMEM((enc, keys), BF), pltpu.VMEM((keys, enc), F32)],
        compiler_params=pltpu.CompilerParams(vmem_limit_bytes=40 * 2**20),
        cost_estimate=pl.CostEstimate(
            flops=7_200_000_000, bytes_accessed=12_000_000, transcendentals=600_000
        ),
    )(states, weights, queries, grad_out)


def place():
    seq = lax.axis_index("seq")
    grp = lax.axis_index("grp")
    return seq // 4, seq % 4, grp // 2, grp % 2


def at(z, x, y, core):
    return {"seq": (z + 8) % 8 * 4 + (x + 4) % 4, "grp": (y + 4) % 4 * 2 + core}


def teammate(z, y, member):
    return at(z, member // 2, y, member % 2)


def greet(friends):
    barrier = pltpu.get_barrier_semaphore()
    for friend in friends:
        pl.semaphore_signal(barrier, inc=1, device_id=friend, device_id_type=MESH)
    pl.semaphore_wait(barrier, len(friends))


def push(src, dst, send_sem, recv_sem, target):
    copy = pltpu.make_async_remote_copy(
        src_ref=src,
        dst_ref=dst,
        send_sem=send_sem,
        recv_sem=recv_sem,
        device_id=target,
        device_id_type=MESH,
    )
    copy.start()
    return copy


def spread_kernel(row_ref, enc_ref, pool_ref, ids_ref, team_sem, row_sem, z_sem, y_sem, own_sem):
    z, x, y, core = place()
    me = x * 2 + core
    friends = [teammate(z, y, (me + k) % 8) for k in range(1, 8)]
    friends += [at(z + k, x, y, core) for k in range(1, 8)]
    friends += [at(z, x, y + k, core) for k in range(1, 4)]
    ids_ref[y, z, me] = row_ref[...]
    greet(friends)
    rows = []
    for k in range(1, 8):
        rows.append(
            push(
                ids_ref.at[y, z, me],
                ids_ref.at[y, z, me],
                row_sem.at[0, k - 1],
                row_sem.at[1, k - 1],
                friends[k - 1],
            )
        )
    pieces = []
    for k in range(1, 8):
        member = (me + k) % 8
        pieces.append(
            push(
                enc_ref.at[:, pl.ds(pl.multiple_of(member * 16, 16), 16), :],
                pool_ref.at[me],
                team_sem.at[0, k - 1],
                team_sem.at[1, k - 1],
                friends[k - 1],
            )
        )
    own = pltpu.make_async_copy(
        enc_ref.at[:, pl.ds(pl.multiple_of(me * 16, 16), 16), :], pool_ref.at[me], own_sem
    )
    own.start()
    for copy in rows:
        copy.wait_recv()
    planes = []
    for k in range(1, 8):
        planes.append(
            push(
                ids_ref.at[y, z],
                ids_ref.at[y, z],
                z_sem.at[0, k - 1],
                z_sem.at[1, k - 1],
                friends[6 + k],
            )
        )
    for copy in planes:
        copy.wait_recv()
    columns = []
    for k in range(1, 4):
        columns.append(
            push(
                ids_ref.at[y],
                ids_ref.at[y],
                y_sem.at[0, k - 1],
                y_sem.at[1, k - 1],
                friends[13 + k],
            )
        )
    own.wait()
    for copy in columns + pieces:
        copy.wait_recv()
    for copy in rows + pieces + planes + columns:
        copy.wait_send()


def spread(row, enc):
    return pl.pallas_call(
        spread_kernel,
        in_specs=[
            pl.BlockSpec(memory_space=pltpu.VMEM),
            pl.BlockSpec(memory_space=pl.ANY),
        ],
        out_specs=[
            pl.BlockSpec(memory_space=pltpu.VMEM),
            pl.BlockSpec(memory_space=pltpu.VMEM),
        ],
        out_shape=[
            jax.ShapeDtypeStruct((8, 8, 16, 512), BF),
            jax.ShapeDtypeStruct((4, 8, 8, 1, 128), jnp.int32),
        ],
        scratch_shapes=[
            pltpu.SemaphoreType.DMA((2, 7)),
            pltpu.SemaphoreType.DMA((2, 7)),
            pltpu.SemaphoreType.DMA((2, 7)),
            pltpu.SemaphoreType.DMA((2, 3)),
            pltpu.SemaphoreType.DMA,
        ],
        compiler_params=pltpu.CompilerParams(
            collective_id=1, has_side_effects=True, vmem_limit_bytes=16 * 2**20
        ),
    )(row, enc)


def starts(caps):
    return [0] + [sum(caps[: r + 1]) for r in range(len(caps))]


def gather_kernel(
    caps, chunk, order_ref, loc_ref, pool_ref, states_ref, packed, arr, stage, ring_sem, team_sem
):
    z, x, y, core = place()
    me = x * 2 + core
    total = sum(caps)
    first = starts(caps)
    friends = [teammate(z, y, (me + k) % 8) for k in range(1, 8)]
    ahead = at(z + 1, x, y, core)
    behind = at(z - 1, x, y, core)
    greet(friends + [ahead, behind])
    copies = {}

    def forward(d, r, i, src):
        slot = first[r] + i * chunk
        index = slot // chunk
        copies[d, r, i] = push(
            src,
            arr.at[pl.ds(d * total + slot, chunk)],
            ring_sem.at[0, d, index],
            ring_sem.at[1, d, index],
            ahead if d == 0 else behind,
        )

    for i in range(caps[0] // chunk):
        for d in range(2):

            def fill(j, carry, i=i, d=d):
                packed[d, i * chunk + j] = pool_ref[order_ref[d, i * chunk + j]]
                return carry

            lax.fori_loop(0, chunk, fill, 0)
            forward(d, 0, i, packed.at[d, pl.ds(i * chunk, chunk)])

    def keep(j, carry):
        arr[2 * total + j] = pool_ref[j]
        return carry

    lax.fori_loop(0, 64, keep, 0)
    for r in range(1, 4):
        for i in range(caps[r] // chunk):
            for d in range(2):
                copies[d, r - 1, i].wait_recv()
                slot = d * total + first[r - 1] + i * chunk
                forward(d, r, i, arr.at[pl.ds(slot, chunk)])
    for r in range(4):
        low = caps[r + 1] // chunk if r < 3 else 0
        for i in range(low, caps[r] // chunk):
            for d in range(2):
                copies[d, r, i].wait_recv()

    def pick(i, carry):
        for k in range(4):
            stage[i, k] = arr[loc_ref[i * 4 + k]]
        return carry

    lax.fori_loop(0, 8, pick, 0)
    rows = pl.ds(pl.multiple_of(me * 16, 16), 16)
    hands = []
    for k in range(1, 8):
        hands.append(
            push(
                stage.at[(me + k) % 8],
                states_ref.at[:, rows, :],
                team_sem.at[0, k - 1],
                team_sem.at[1, k - 1],
                friends[k - 1],
            )
        )
    states_ref[:, rows, :] = stage[me]
    for copy in hands:
        copy.wait_recv()
    for copy in hands + list(copies.values()):
        copy.wait_send()


def gather(caps, chunk, number, order, loc, pool):
    total = sum(caps)
    return pl.pallas_call(
        functools.partial(gather_kernel, caps, chunk),
        in_specs=[
            pl.BlockSpec(memory_space=pltpu.SMEM),
            pl.BlockSpec(memory_space=pltpu.SMEM),
            pl.BlockSpec(memory_space=pltpu.VMEM),
        ],
        out_specs=pl.BlockSpec(memory_space=pltpu.VMEM),
        out_shape=jax.ShapeDtypeStruct((4, 128, 512), BF),
        scratch_shapes=[
            pltpu.VMEM((2, caps[0], 16, 512), BF),
            pltpu.VMEM((2 * total + 64, 16, 512), BF),
            pltpu.VMEM((8, 4, 16, 512), BF),
            pltpu.SemaphoreType.DMA((2, 2, total // chunk)),
            pltpu.SemaphoreType.DMA((2, 7)),
        ],
        compiler_params=pltpu.CompilerParams(
            collective_id=number, has_side_effects=True, vmem_limit_bytes=24 * 2**20
        ),
    )(order, loc, pool)


def finish_kernel(
    caps,
    chunk,
    mate_ref,
    con_ref,
    fin_ref,
    ge_ref,
    dw_ref,
    gs_ref,
    gw_ref,
    taken,
    comb,
    outb,
    inb,
    done,
    pair_in,
    held,
    y_half,
    y_in,
    x_half,
    x_in,
    z_in,
    team_sem,
    ring_sem,
    home_sem,
    core_sem,
    y_sem,
    x_sem,
    z_sem,
):
    z, x, y, core = place()
    me = x * 2 + core
    total = sum(caps)
    first = starts(caps)
    friends = [teammate(z, y, (me + k) % 8) for k in range(1, 8)]
    around = [at(z + k, x, y, core) for k in range(1, 8)]
    ahead = around[0]
    behind = around[6]
    sides = [at(z, x, y + 1, core), at(z, x, y - 1, core)]
    greet(friends + around + sides)

    def send(src, dst, sems, slot, target):
        return push(src, dst, sems.at[0, slot], sems.at[1, slot], target)

    given = []
    for k in range(1, 8):
        member = (me + k) % 8
        given.append(
            send(
                ge_ref.at[:, pl.ds(pl.multiple_of(member * 16, 16), 16), :],
                taken.at[pl.ds(me * 4, 4)],
                team_sem,
                k - 1,
                friends[k - 1],
            )
        )
    offsets = (2, 1, 3, 0)
    partner = at(z, x, y, 1 - core)
    swaps = []
    for slot, offset in enumerate(offsets):
        theirs = (y + offset) % 4 * 2 + 1 - core
        swaps.append(send(dw_ref.at[theirs], pair_in.at[slot], core_sem, slot, partner))
    taken[pl.ds(me * 4, 4)] = ge_ref[:, pl.ds(pl.multiple_of(me * 16, 16), 16), :]
    taken[32] = jnp.zeros((16, 512), BF)
    comb[32] = jnp.zeros((16, 512), F32)
    inb[2 * total] = jnp.zeros((16, 512), BF)
    for copy in given:
        copy.wait_recv()

    def combine(i, carry):
        row = taken[mate_ref[i, 0]].astype(F32)
        for t in range(1, 4):
            row = row + taken[mate_ref[i, t]].astype(F32)
        comb[i] = row
        return carry

    lax.fori_loop(0, 32, combine, 0)
    copies = {}

    def back(r, i, added):
        for d in range(2):
            slot = d * total + first[r] + i * chunk
            if added:
                copies[d, r + 1, i].wait_recv()
                further = d * total + first[r + 1] + i * chunk

                def fill(j, carry, d=d, slot=slot, further=further):
                    outb[slot + j] = (
                        comb[con_ref[d, r, i * chunk + j]] + inb[further + j].astype(F32)
                    ).astype(BF)
                    return carry
            else:

                def fill(j, carry, d=d, slot=slot):
                    outb[slot + j] = comb[con_ref[d, r, i * chunk + j]].astype(BF)
                    return carry

            lax.fori_loop(0, chunk, fill, 0)
            index = (first[r] + i * chunk) // chunk
            copies[d, r, i] = push(
                outb.at[pl.ds(slot, chunk)],
                inb.at[pl.ds(slot, chunk)],
                ring_sem.at[0, d, index],
                ring_sem.at[1, d, index],
                behind if d == 0 else ahead,
            )

    for i in range(caps[3] // chunk):
        back(3, i, False)
    for r in (2, 1, 0):
        for i in range(caps[r + 1] // chunk, caps[r] // chunk):
            back(r, i, False)

    def add_pair(slot, offset):
        swaps[slot].wait_recv()
        mine = (y + offset) % 4 * 2 + core
        for part in range(4):
            held[slot, part] = (
                dw_ref[mine, part].astype(F32) + pair_in[slot, part].astype(F32)
            ).astype(BF)

    add_pair(0, 2)
    up = send(held.at[0, pl.ds(0, 2)], y_half.at[0], y_sem, 0, sides[0])
    down = send(held.at[0, pl.ds(2, 2)], y_half.at[1], y_sem, 1, sides[1])
    for i in range(caps[3] // chunk):
        back(2, i, True)
    add_pair(1, 1)
    add_pair(2, 3)
    add_pair(3, 0)
    for i in range(caps[2] // chunk):
        back(1, i, True)
    up.wait_recv()
    for part in range(2):
        held[1, part] = (held[1, part].astype(F32) + y_half[0, part].astype(F32)).astype(BF)
    up2 = send(held.at[1], y_in.at[0], y_sem, 2, sides[0])
    down.wait_recv()
    for part in range(2):
        held[2, part + 2] = (
            held[2, part + 2].astype(F32) + y_half[1, part].astype(F32)
        ).astype(BF)
    down2 = send(held.at[2], y_in.at[1], y_sem, 3, sides[1])
    for i in range(caps[1] // chunk):
        back(0, i, True)
    for i in range(caps[0] // chunk):
        for d in range(2):
            copies[d, 0, i].wait_recv()

    def close(i, carry):
        for k in range(8):
            b = i * 8 + k
            done[i, k] = (
                inb[fin_ref[b, 0]].astype(F32)
                + inb[fin_ref[b, 1]].astype(F32)
                + comb[fin_ref[b, 2]]
            ).astype(BF)
        return carry

    lax.fori_loop(0, 8, close, 0)
    rows = pl.ds(pl.multiple_of(me * 16, 16), 16)
    homes = []
    for k in range(1, 8):
        homes.append(
            send(
                done.at[(me + k) % 8],
                gs_ref.at[:, rows, :],
                home_sem,
                k - 1,
                friends[k - 1],
            )
        )
    gs_ref[:, rows, :] = done[me]
    up2.wait_recv()
    down2.wait_recv()

    def y_total(offset):
        part = (x + offset) % 4
        return (
            held[3, part].astype(F32)
            + y_in[0, part].astype(F32)
            + y_in[1, part].astype(F32)
        )

    left = at(z, x - 1, y, core)
    right = at(z, x + 1, y, core)
    held[4, 0] = y_total(2).astype(BF)
    xup = send(held.at[4, 0, 0], x_half.at[0], x_sem, 0, right)
    xdown = send(held.at[4, 0, 1], x_half.at[1], x_sem, 1, left)
    ahead_x = y_total(1)
    behind_x = y_total(3)
    own = y_total(0)
    xup.wait_recv()
    held[4, 1, 0] = (ahead_x[0] + x_half[0].astype(F32)).astype(BF)
    held[4, 1, 1] = ahead_x[1].astype(BF)
    xup2 = send(held.at[4, 1], x_in.at[0], x_sem, 2, right)
    xdown.wait_recv()
    held[4, 2, 0] = behind_x[0].astype(BF)
    held[4, 2, 1] = (behind_x[1] + x_half[1].astype(F32)).astype(BF)
    xdown2 = send(held.at[4, 2], x_in.at[1], x_sem, 3, left)
    xup2.wait_recv()
    xdown2.wait_recv()
    held[4, 3] = (own + x_in[0].astype(F32) + x_in[1].astype(F32)).astype(BF)

    zs = []
    for step in (4, 3, 5, 2, 6, 1, 7):
        target = (z + step) % 8
        zs.append(
            send(held.at[4, 3, :, target], z_in.at[step - 1], z_sem, step - 1, around[step - 1])
        )
    result = held[4, 3, :, z].astype(F32)
    for copy, step in zip(zs, (4, 3, 5, 2, 6, 1, 7)):
        copy.wait_recv()
        result = result + z_in[step - 1].astype(F32)
    gw_ref[...] = result
    for copy in homes:
        copy.wait_recv()
    rest = swaps + [up, down, up2, down2, xup, xdown, xup2, xdown2] + zs
    for copy in given + homes + rest + list(copies.values()):
        copy.wait_send()


def finish(caps, chunk, number, mate, con, fin, ge, dw):
    total = sum(caps)
    smem = pl.BlockSpec(memory_space=pltpu.SMEM)
    vmem = pl.BlockSpec(memory_space=pltpu.VMEM)
    return pl.pallas_call(
        functools.partial(finish_kernel, caps, chunk),
        in_specs=[smem, smem, smem, vmem, vmem],
        out_specs=[vmem, vmem],
        out_shape=[
            jax.ShapeDtypeStruct((8, 128, 512), BF),
            jax.ShapeDtypeStruct((2, 16, 256), F32),
        ],
        scratch_shapes=[
            pltpu.VMEM((33, 16, 512), BF),
            pltpu.VMEM((33, 16, 512), F32),
            pltpu.VMEM((2 * total, 16, 512), BF),
            pltpu.VMEM((2 * total + 1, 16, 512), BF),
            pltpu.VMEM((8, 8, 16, 512), BF),
            pltpu.VMEM((4, 4, 2, 8, 16, 256), BF),
            pltpu.VMEM((5, 4, 2, 8, 16, 256), BF),
            pltpu.VMEM((2, 2, 2, 8, 16, 256), BF),
            pltpu.VMEM((2, 4, 2, 8, 16, 256), BF),
            pltpu.VMEM((2, 8, 16, 256), BF),
            pltpu.VMEM((2, 2, 8, 16, 256), BF),
            pltpu.VMEM((7, 2, 16, 256), BF),
            pltpu.SemaphoreType.DMA((2, 7)),
            pltpu.SemaphoreType.DMA((2, 2, total // chunk)),
            pltpu.SemaphoreType.DMA((2, 7)),
            pltpu.SemaphoreType.DMA((2, 4)),
            pltpu.SemaphoreType.DMA((2, 4)),
            pltpu.SemaphoreType.DMA((2, 4)),
            pltpu.SemaphoreType.DMA((2, 7)),
        ],
        compiler_params=pltpu.CompilerParams(
            collective_id=number, has_side_effects=True, vmem_limit_bytes=48 * 2**20
        ),
    )(mate, con, fin, ge, dw)


TIGHT = (24, 20, 16, 8)
WIDE = (64, 64, 64, 32)


def plan(ids):
    z, x, y, core = place()
    i32 = jnp.int32
    member_core = jnp.arange(8, dtype=i32)[None, None, :, None] % 2
    block = (ids // 8 % 4 * 2 + member_core) * 8 + ids % 8
    owner_z = ids // 32
    away = (jnp.arange(8, dtype=i32)[None, :, None, None] - owner_z + 8) % 8
    flat = (owner_z * 64 + block).reshape(4, 256)
    is_block = (flat[:, None, :] == jnp.arange(512, dtype=i32)[None, :, None]).astype(BF)
    is_away = (away.reshape(4, 1, 256) == jnp.arange(8, dtype=i32)[None, :, None]).astype(BF)
    wanted = jnp.einsum("ydr,ybr->ydb", is_away, is_block, preferred_element_type=F32) > 0.5
    wanted = wanted.reshape(4, 8, 8, 64)
    team = jnp.arange(64, dtype=i32)
    even = team % 2 == 0

    def far(one, two, three, four):
        return jnp.where(four, 4, jnp.where(three, 3, jnp.where(two, 2, jnp.where(one, 1, 0))))

    up = far(wanted[:, 1], wanted[:, 2], wanted[:, 3], wanted[:, 4] & even)
    down = far(wanted[:, 7], wanted[:, 6], wanted[:, 5], wanted[:, 4] & ~even)
    fars = jnp.stack([up, down], axis=1).astype(i32)
    lengths = jnp.stack(
        [jnp.max(jnp.sum((fars >= r).astype(i32), axis=-1)) for r in range(1, 5)]
    )
    fits = jnp.all(lengths <= jnp.array(TIGHT, i32))
    fars = lax.dynamic_index_in_dim(fars, y, 0, keepdims=False)
    fars = lax.dynamic_slice_in_dim(jnp.concatenate([fars, fars], axis=1), z, 8, axis=1)
    key = fars * 64 + 63 - team
    rank = jnp.sum((key[..., None, :] > key[..., :, None]).astype(i32), axis=-1)
    at_rank = rank[..., None, :] == team[:, None]
    order = jnp.sum(jnp.where(at_rank[:, 0], team, 0), axis=-1)

    def mine(a):
        a = lax.dynamic_index_in_dim(a, y, 0, keepdims=False)
        return lax.dynamic_index_in_dim(a, z, 0, keepdims=False).reshape(32)

    my_block, my_away = mine(block), mine(away)
    my_flat = (8 - my_away) % 8 * 64 + my_block
    upwards = (my_away < 4) | ((my_away == 4) & (my_block % 2 == 0))
    hops = jnp.where(upwards, my_away, 8 - my_away)
    hit = my_flat[:, None] == jnp.arange(512, dtype=i32)[None, :]
    ranks = jnp.sum(jnp.where(hit[None], rank.reshape(2, 1, 512), 0), axis=-1)
    spot = jnp.where(upwards, ranks[0], ranks[1])
    refs = jnp.arange(32, dtype=i32)
    first = jnp.min(jnp.where(hit, refs[:, None], 32), axis=0).reshape(8, 64)
    same = my_flat[:, None] == my_flat[None, :]
    earlier = jnp.sum((same[:, None, :] & (refs[None, None, :] < refs[None, :, None])).astype(i32), axis=-1)
    mate = 32 + jnp.sum(
        jnp.where(
            same[:, None, :] & (earlier[:, None, :] == jnp.arange(4, dtype=i32)[None, :, None]),
            refs - 32,
            0,
        ),
        axis=-1,
    )
    firsts = jnp.stack(
        [
            jnp.stack([first[7], first[6], first[5], jnp.where(even, first[4], 32)]),
            jnp.stack([first[1], first[2], first[3], jnp.where(even, 32, first[4])]),
        ]
    )
    at_rank_by_hop = jnp.stack(
        [
            jnp.stack([at_rank[0, 7], at_rank[0, 6], at_rank[0, 5], at_rank[0, 4]]),
            jnp.stack([at_rank[1, 1], at_rank[1, 2], at_rank[1, 3], at_rank[1, 4]]),
        ]
    )
    con = 32 + jnp.sum(jnp.where(at_rank_by_hop, firsts[:, :, None, :] - 32, 0), axis=-1)

    def locate(caps):
        total = sum(caps)
        offset = sum(jnp.where(hops == r + 1, starts(caps)[r], 0) for r in range(4))
        there = jnp.where(upwards, 0, total) + offset + spot
        return jnp.where(my_away == 0, 2 * total + my_block, there)

    def collect(caps):
        total = sum(caps)
        return jnp.stack(
            [
                jnp.where(fars[0, 0] > 0, rank[0, 0], 2 * total),
                jnp.where(fars[1, 0] > 0, total + rank[1, 0], 2 * total),
                first[0],
            ],
            axis=1,
        )

    return fits, order, mate, con, locate, collect


def body(queries, grad_out, enc_states, neighbour_ids, kv_weight):
    row = jnp.pad(neighbour_ids.reshape(1, 4), ((0, 0), (0, 124)))
    pool, ids = spread(row, enc_states[0])
    fits, order, mate, con, locate, collect = plan(ids[:, :, :, 0, :4])
    pool = pool.reshape(64, 16, 512)
    states = lax.cond(
        fits,
        lambda: gather(TIGHT, 4, 2, order, locate(TIGHT), pool),
        lambda: gather(WIDE, 16, 3, order, locate(WIDE), pool),
    )
    gq, grad_e, dw = attention(states.reshape(512, 512), kv_weight, queries[0], grad_out[0])
    grad_e = grad_e.reshape(4, 128, 512)
    grad_states, grad_weight = lax.cond(
        fits,
        lambda: finish(TIGHT, 4, 4, mate, con, collect(TIGHT), grad_e, dw),
        lambda: finish(WIDE, 16, 5, mate, con, collect(WIDE), grad_e, dw),
    )
    return (gq[None], grad_states[None], grad_weight)


def solution(mesh):
    placed = (
        P("grp", "seq", None),
        P("grp", "seq", None),
        P("grp", "seq", None, None),
        P("grp", "seq", None),
        P(),
    )
    return jax.shard_map(
        body,
        mesh=mesh,
        in_specs=placed,
        out_specs=(P("grp", "seq", None), P("grp", "seq", None, None), P(None, "seq", "grp")),
        check_vma=False,
    )
```

```python
import functools
import math

import jax
import jax.numpy as jnp
from jax import lax
from jax.experimental import pallas as pl
from jax.experimental.pallas import tpu as pltpu
from jax.sharding import PartitionSpec as P

DH = 128
BF = jnp.bfloat16
F32 = jnp.float32
MESH = pl.DeviceIdType.MESH
NT = (((1,), (1,)), ((), ()))
TN = (((0,), (0,)), ((), ()))


def attention_kernel(states_ref, w_ref, q_ref, go_ref, gq_ref, ge_ref, dw_ref, st_ref, acc_ref):
    step = pl.program_id(0)
    scale = 1.0 / math.sqrt(DH)

    @pl.when(step == 0)
    def _():
        st_ref[...] = states_ref[...].T
        acc_ref[...] = jnp.zeros_like(acc_ref)

    states = states_ref[...]
    wk = w_ref[0]
    wv = w_ref[1]
    keys = jnp.dot(states, wk, preferred_element_type=F32).astype(BF)
    values = jnp.dot(states, wv, preferred_element_type=F32).astype(BF)
    blank = jnp.zeros((64, DH), BF)
    gk_parts = []
    gv_parts = []
    for span in range(2):
        q = q_ref[span * 64 : span * 64 + 64, :]
        go = go_ref[span * 64 : span * 64 + 64, :]
        key = keys[span * 256 : span * 256 + 256, :]
        value = values[span * 256 : span * 256 + 256, :]
        qd = jnp.concatenate(
            [
                jnp.concatenate([q[:, :DH], blank], axis=1),
                jnp.concatenate([blank, q[:, DH:]], axis=1),
            ],
            axis=0,
        )
        gd = jnp.concatenate(
            [
                jnp.concatenate([go[:, :DH], blank], axis=1),
                jnp.concatenate([blank, go[:, DH:]], axis=1),
            ],
            axis=0,
        )
        scores = lax.dot_general(key, qd, NT, preferred_element_type=F32) * scale
        top = jnp.max(scores, axis=0, keepdims=True)
        expo = jnp.exp(scores - top)
        weights = expo / jnp.sum(expo, axis=0, keepdims=True)
        weights_b = weights.astype(BF)
        gp = lax.dot_general(value, gd, NT, preferred_element_type=F32)
        delta = jnp.sum(weights_b.astype(F32) * gp, axis=0, keepdims=True)
        gs = (weights * (gp - delta) * scale).astype(BF)
        gv_parts.append(jnp.dot(weights_b, gd, preferred_element_type=F32).astype(BF))
        gk_parts.append(jnp.dot(gs, qd, preferred_element_type=F32).astype(BF))
        gq = lax.dot_general(gs, key, TN, preferred_element_type=F32).astype(BF)
        gq_ref[span * 64 : span * 64 + 64, :DH] = gq[:64, :DH]
        gq_ref[span * 64 : span * 64 + 64, DH:] = gq[64:, DH:]
    gk = jnp.concatenate(gk_parts, axis=0)
    gv = jnp.concatenate(gv_parts, axis=0)
    total = acc_ref[...]
    total = total + lax.dot_general(gk, wk, NT, preferred_element_type=F32)
    total = total + lax.dot_general(gv, wv, NT, preferred_element_type=F32)
    acc_ref[...] = total

    @pl.when(step == pl.num_programs(0) - 1)
    def _():
        ge_ref[...] = total.astype(BF)

    turned = st_ref[...]
    for kind, part in enumerate((gk, gv)):
        share = jnp.dot(turned, part, preferred_element_type=F32).astype(BF)
        for z in range(8):
            for x in range(4):
                row = (z * 4 + x) * 16
                dw_ref[0, x, kind, z] = share[row : row + 16, :]


def attention(states, weights, queries, grad_out):
    keys, enc = states.shape
    tokens, width = queries.shape
    return pl.pallas_call(
        attention_kernel,
        grid=(8,),
        in_specs=[
            pl.BlockSpec((keys, enc), lambda i: (0, 0)),
            pl.BlockSpec((2, enc, 256), lambda i: (0, 0, i)),
            pl.BlockSpec((tokens, 256), lambda i: (0, i)),
            pl.BlockSpec((tokens, 256), lambda i: (0, i)),
        ],
        out_specs=[
            pl.BlockSpec((tokens, 256), lambda i: (0, i)),
            pl.BlockSpec((keys, enc), lambda i: (0, 0)),
            pl.BlockSpec((1, 4, 2, 8, 16, 256), lambda i: (i, 0, 0, 0, 0, 0)),
        ],
        out_shape=[
            jax.ShapeDtypeStruct((tokens, width), BF),
            jax.ShapeDtypeStruct((keys, enc), BF),
            jax.ShapeDtypeStruct((8, 4, 2, 8, 16, 256), BF),
        ],
        scratch_shapes=[pltpu.VMEM((enc, keys), BF), pltpu.VMEM((keys, enc), F32)],
        compiler_params=pltpu.CompilerParams(vmem_limit_bytes=60 * 2**20),
        cost_estimate=pl.CostEstimate(
            flops=7_200_000_000, bytes_accessed=12_000_000, transcendentals=600_000
        ),
    )(states, weights, queries, grad_out)


def place():
    seq = lax.axis_index("seq")
    grp = lax.axis_index("grp")
    return seq // 4, seq % 4, grp // 2, grp % 2


def at(z, x, y, core):
    return {"seq": (z + 8) % 8 * 4 + (x + 4) % 4, "grp": (y + 4) % 4 * 2 + core}


def teammate(z, y, member):
    return at(z, member // 2, y, member % 2)


def greet(friends):
    barrier = pltpu.get_barrier_semaphore()
    for friend in friends:
        pl.semaphore_signal(barrier, inc=1, device_id=friend, device_id_type=MESH)
    pl.semaphore_wait(barrier, len(friends))


def push(src, dst, send_sem, recv_sem, target):
    copy = pltpu.make_async_remote_copy(
        src_ref=src,
        dst_ref=dst,
        send_sem=send_sem,
        recv_sem=recv_sem,
        device_id=target,
        device_id_type=MESH,
    )
    copy.start()
    return copy


def spread_kernel(row_ref, enc_ref, pool_ref, ids_ref, team_sem, row_sem, z_sem, y_sem, own_sem):
    z, x, y, core = place()
    me = x * 2 + core
    friends = [teammate(z, y, (me + k) % 8) for k in range(1, 8)]
    friends += [at(z + k, x, y, core) for k in range(1, 8)]
    friends += [at(z, x, y + k, core) for k in range(1, 4)]
    ids_ref[y, z, me] = row_ref[...]
    greet(friends)
    rows = []
    for k in range(1, 8):
        rows.append(
            push(
                ids_ref.at[y, z, me],
                ids_ref.at[y, z, me],
                row_sem.at[0, k - 1],
                row_sem.at[1, k - 1],
                friends[k - 1],
            )
        )
    pieces = []
    for k in range(1, 8):
        member = (me + k) % 8
        pieces.append(
            push(
                enc_ref.at[:, pl.ds(pl.multiple_of(member * 16, 16), 16), pl.ds(0, 256)],
                pool_ref.at[me],
                team_sem.at[0, k - 1],
                team_sem.at[1, k - 1],
                friends[k - 1],
            )
        )
    own = pltpu.make_async_copy(
        enc_ref.at[:, pl.ds(pl.multiple_of(me * 16, 16), 16), pl.ds(0, 256)],
        pool_ref.at[me],
        own_sem,
    )
    own.start()
    for copy in rows:
        copy.wait_recv()
    planes = []
    for k in range(1, 8):
        planes.append(
            push(
                ids_ref.at[y, z],
                ids_ref.at[y, z],
                z_sem.at[0, k - 1],
                z_sem.at[1, k - 1],
                friends[6 + k],
            )
        )
    for copy in planes:
        copy.wait_recv()
    columns = []
    for k in range(1, 4):
        columns.append(
            push(
                ids_ref.at[y],
                ids_ref.at[y],
                y_sem.at[0, k - 1],
                y_sem.at[1, k - 1],
                friends[13 + k],
            )
        )
    own.wait()
    for copy in columns + pieces:
        copy.wait_recv()
    for copy in rows + pieces + planes + columns:
        copy.wait_send()


def spread(row, enc):
    return pl.pallas_call(
        spread_kernel,
        in_specs=[
            pl.BlockSpec(memory_space=pltpu.VMEM),
            pl.BlockSpec(memory_space=pl.ANY),
        ],
        out_specs=[
            pl.BlockSpec(memory_space=pltpu.VMEM),
            pl.BlockSpec(memory_space=pltpu.VMEM),
        ],
        out_shape=[
            jax.ShapeDtypeStruct((8, 8, 16, 256), BF),
            jax.ShapeDtypeStruct((4, 8, 8, 1, 128), jnp.int32),
        ],
        scratch_shapes=[
            pltpu.SemaphoreType.DMA((2, 7)),
            pltpu.SemaphoreType.DMA((2, 7)),
            pltpu.SemaphoreType.DMA((2, 7)),
            pltpu.SemaphoreType.DMA((2, 3)),
            pltpu.SemaphoreType.DMA,
        ],
        compiler_params=pltpu.CompilerParams(
            collective_id=1, has_side_effects=True, vmem_limit_bytes=16 * 2**20
        ),
    )(row, enc)


def starts(caps):
    return [0] + [sum(caps[: r + 1]) for r in range(len(caps))]


def gather_kernel(
    caps,
    chunk,
    order_ref,
    loc_ref,
    pool_ref,
    enc_ref,
    states_ref,
    pool1,
    packed,
    arr0,
    arr1,
    stage0,
    stage1,
    ring_sem,
    team_sem,
    spread_sem,
    own_sem,
):
    z, x, y, core = place()
    me = x * 2 + core
    total = sum(caps)
    first = starts(caps)
    friends = [teammate(z, y, (me + k) % 8) for k in range(1, 8)]
    ahead = at(z + 1, x, y, core)
    behind = at(z - 1, x, y, core)
    own = pltpu.make_async_copy(
        enc_ref.at[:, pl.ds(pl.multiple_of(me * 16, 16), 16), pl.ds(256, 256)],
        pool1.at[pl.ds(pl.multiple_of(me * 8, 8), 8)],
        own_sem,
    )
    own.start()
    greet(friends + [ahead, behind])
    copies = {}
    arrs = (arr0, arr1)
    stages = (stage0, stage1)

    def forward(h, d, r, i, src):
        slot = first[r] + i * chunk
        index = slot // chunk
        copies[h, d, r, i] = push(
            src,
            arrs[h].at[pl.ds(d * total + slot, chunk)],
            ring_sem.at[0, h, d, index],
            ring_sem.at[1, h, d, index],
            ahead if d == 0 else behind,
        )

    def first_hop(h, pool):
        for i in range(caps[0] // chunk):
            for d in range(2):

                def fill(j, carry, i=i, d=d):
                    packed[h, d, i * chunk + j] = pool[order_ref[d, i * chunk + j]]
                    return carry

                lax.fori_loop(0, chunk, fill, 0, unroll=4)
                forward(h, d, 0, i, packed.at[h, d, pl.ds(i * chunk, chunk)])

        def keep(j, carry):
            arrs[h][2 * total + j] = pool[j]
            return carry

        lax.fori_loop(0, 64, keep, 0, unroll=8)

    def next_hop(h, r):
        for i in range(caps[r] // chunk):
            for d in range(2):
                copies[h, d, r - 1, i].wait_recv()
                slot = d * total + first[r - 1] + i * chunk
                forward(h, d, r, i, arrs[h].at[pl.ds(slot, chunk)])

    rows = pl.ds(pl.multiple_of(me * 16, 16), 16)
    hands = []

    def hand_out(h):
        for r in range(4):
            low = caps[r + 1] // chunk if r < 3 else 0
            for i in range(low, caps[r] // chunk):
                for d in range(2):
                    copies[h, d, r, i].wait_recv()

        def pick(i, carry):
            for k in range(4):
                stages[h][i, k] = arrs[h][loc_ref[i * 4 + k]]
            return carry

        lax.fori_loop(0, 8, pick, 0)
        for k in range(1, 8):
            hands.append(
                push(
                    stages[h].at[(me + k) % 8],
                    states_ref.at[:, rows, pl.ds(h * 256, 256)],
                    team_sem.at[0, h, k - 1],
                    team_sem.at[1, h, k - 1],
                    friends[k - 1],
                )
            )
        states_ref[:, rows, h * 256 : h * 256 + 256] = stages[h][me]

    first_hop(0, pool_ref)
    pieces = []
    for k in range(1, 8):
        member = (me + k) % 8
        pieces.append(
            push(
                enc_ref.at[:, pl.ds(pl.multiple_of(member * 16, 16), 16), pl.ds(256, 256)],
                pool1.at[pl.ds(pl.multiple_of(me * 8, 8), 8)],
                spread_sem.at[0, k - 1],
                spread_sem.at[1, k - 1],
                friends[k - 1],
            )
        )
    next_hop(0, 1)
    own.wait()
    for copy in pieces:
        copy.wait_recv()
    first_hop(1, pool1)
    next_hop(0, 2)
    next_hop(0, 3)
    next_hop(1, 1)
    hand_out(0)
    next_hop(1, 2)
    next_hop(1, 3)
    hand_out(1)
    for copy in hands:
        copy.wait_recv()
    for copy in hands + pieces + list(copies.values()):
        copy.wait_send()


def gather(caps, chunk, number, order, loc, pool, enc):
    total = sum(caps)
    return pl.pallas_call(
        functools.partial(gather_kernel, caps, chunk),
        in_specs=[
            pl.BlockSpec(memory_space=pltpu.SMEM),
            pl.BlockSpec(memory_space=pltpu.SMEM),
            pl.BlockSpec(memory_space=pltpu.VMEM),
            pl.BlockSpec(memory_space=pl.ANY),
        ],
        out_specs=pl.BlockSpec(memory_space=pltpu.VMEM),
        out_shape=jax.ShapeDtypeStruct((4, 128, 512), BF),
        scratch_shapes=[
            pltpu.VMEM((64, 16, 256), BF),
            pltpu.VMEM((2, 2, caps[0], 16, 256), BF),
            pltpu.VMEM((2 * total + 64, 16, 256), BF),
            pltpu.VMEM((2 * total + 64, 16, 256), BF),
            pltpu.VMEM((8, 4, 16, 256), BF),
            pltpu.VMEM((8, 4, 16, 256), BF),
            pltpu.SemaphoreType.DMA((2, 2, 2, total // chunk)),
            pltpu.SemaphoreType.DMA((2, 2, 7)),
            pltpu.SemaphoreType.DMA((2, 7)),
            pltpu.SemaphoreType.DMA,
        ],
        compiler_params=pltpu.CompilerParams(
            collective_id=number, has_side_effects=True, vmem_limit_bytes=24 * 2**20
        ),
    )(order, loc, pool, enc)


def finish_kernel(
    caps,
    chunk,
    mate_ref,
    con_ref,
    fin_ref,
    ge_ref,
    dw_ref,
    gs_ref,
    gw_ref,
    taken0,
    taken1,
    comb0,
    comb1,
    outb,
    inb0,
    inb1,
    done,
    pair_in,
    held,
    y_half,
    y_in,
    x_half,
    x_in,
    z_in,
    team_sem,
    ring_sem,
    home_sem,
    core_sem,
    y_sem,
    x_sem,
    z_sem,
):
    z, x, y, core = place()
    me = x * 2 + core
    total = sum(caps)
    first = starts(caps)
    friends = [teammate(z, y, (me + k) % 8) for k in range(1, 8)]
    around = [at(z + k, x, y, core) for k in range(1, 8)]
    ahead = around[0]
    behind = around[6]
    sides = [at(z, x, y + 1, core), at(z, x, y - 1, core)]
    greet(friends + around + sides)

    def send(src, dst, sems, slot, target):
        return push(src, dst, sems.at[0, slot], sems.at[1, slot], target)

    takens = (taken0, taken1)
    combs = (comb0, comb1)
    inbs = (inb0, inb1)
    given = []

    def give(h):
        for k in range(1, 8):
            member = (me + k) % 8
            given.append(
                push(
                    ge_ref.at[
                        :, pl.ds(pl.multiple_of(member * 16, 16), 16), pl.ds(h * 256, 256)
                    ],
                    takens[h].at[pl.ds(me * 4, 4)],
                    team_sem.at[0, h, k - 1],
                    team_sem.at[1, h, k - 1],
                    friends[k - 1],
                )
            )

    give(0)
    offsets = (2, 1, 3, 0)
    partner = at(z, x, y, 1 - core)
    swaps = []
    for slot, offset in enumerate(offsets):
        theirs = (y + offset) % 4 * 2 + 1 - core
        swaps.append(send(dw_ref.at[theirs], pair_in.at[slot], core_sem, slot, partner))
    give(1)

    def combine(h):
        taken, comb = takens[h], combs[h]
        mine = pl.ds(pl.multiple_of(me * 16, 16), 16)
        taken[pl.ds(me * 4, 4)] = ge_ref[:, mine, h * 256 : h * 256 + 256]
        taken[32] = jnp.zeros((16, 256), BF)
        comb[32] = jnp.zeros((16, 256), F32)
        inbs[h][2 * total] = jnp.zeros((16, 256), BF)
        for copy in given[h * 7 : h * 7 + 7]:
            copy.wait_recv()

        def step(i, carry):
            row = taken[mate_ref[i, 0]].astype(F32)
            for t in range(1, 4):
                row = row + taken[mate_ref[i, t]].astype(F32)
            comb[i] = row
            return carry

        lax.fori_loop(0, 32, step, 0, unroll=4)

    copies = {}

    def back(h, r, i, added):
        comb, inb = combs[h], inbs[h]
        for d in range(2):
            slot = d * total + first[r] + i * chunk
            if added:
                copies[h, d, r + 1, i].wait_recv()
                further = d * total + first[r + 1] + i * chunk

                def fill(j, carry, d=d, slot=slot, further=further):
                    outb[h, slot + j] = (
                        comb[con_ref[d, r, i * chunk + j]] + inb[further + j].astype(F32)
                    ).astype(BF)
                    return carry
            else:

                def fill(j, carry, d=d, slot=slot):
                    outb[h, slot + j] = comb[con_ref[d, r, i * chunk + j]].astype(BF)
                    return carry

            lax.fori_loop(0, chunk, fill, 0, unroll=4)
            index = (first[r] + i * chunk) // chunk
            copies[h, d, r, i] = push(
                outb.at[h, pl.ds(slot, chunk)],
                inb.at[pl.ds(slot, chunk)],
                ring_sem.at[0, h, d, index],
                ring_sem.at[1, h, d, index],
                behind if d == 0 else ahead,
            )

    def farthest(h):
        for i in range(caps[3] // chunk):
            back(h, 3, i, False)
        for r in (2, 1, 0):
            for i in range(caps[r + 1] // chunk, caps[r] // chunk):
                back(h, r, i, False)

    def nearer(h, r):
        for i in range(caps[r + 1] // chunk):
            back(h, r, i, True)

    rows = pl.ds(pl.multiple_of(me * 16, 16), 16)
    homes = []

    def go_home(h):
        comb, inb = combs[h], inbs[h]
        for i in range(caps[0] // chunk):
            for d in range(2):
                copies[h, d, 0, i].wait_recv()

        def close(i, carry):
            for k in range(8):
                b = i * 8 + k
                done[h, i, k] = (
                    inb[fin_ref[b, 0]].astype(F32)
                    + inb[fin_ref[b, 1]].astype(F32)
                    + comb[fin_ref[b, 2]]
                ).astype(BF)
            return carry

        lax.fori_loop(0, 8, close, 0)
        for k in range(1, 8):
            homes.append(
                push(
                    done.at[h, (me + k) % 8],
                    gs_ref.at[:, rows, pl.ds(h * 256, 256)],
                    home_sem.at[0, h, k - 1],
                    home_sem.at[1, h, k - 1],
                    friends[k - 1],
                )
            )
        gs_ref[:, rows, h * 256 : h * 256 + 256] = done[h, me]

    def add_pair(slot, offset):
        swaps[slot].wait_recv()
        mine = (y + offset) % 4 * 2 + core
        for part in range(4):
            held[slot, part] = (
                dw_ref[mine, part].astype(F32) + pair_in[slot, part].astype(F32)
            ).astype(BF)

    combine(0)
    farthest(0)
    add_pair(0, 2)
    up = send(held.at[0, pl.ds(0, 2)], y_half.at[0], y_sem, 0, sides[0])
    down = send(held.at[0, pl.ds(2, 2)], y_half.at[1], y_sem, 1, sides[1])
    nearer(0, 2)
    combine(1)
    farthest(1)
    add_pair(1, 1)
    nearer(0, 1)
    add_pair(2, 3)
    add_pair(3, 0)
    nearer(0, 0)
    up.wait_recv()
    for part in range(2):
        held[1, part] = (held[1, part].astype(F32) + y_half[0, part].astype(F32)).astype(BF)
    up2 = send(held.at[1], y_in.at[0], y_sem, 2, sides[0])
    down.wait_recv()
    for part in range(2):
        held[2, part + 2] = (
            held[2, part + 2].astype(F32) + y_half[1, part].astype(F32)
        ).astype(BF)
    down2 = send(held.at[2], y_in.at[1], y_sem, 3, sides[1])
    nearer(1, 2)
    go_home(0)
    nearer(1, 1)
    up2.wait_recv()
    down2.wait_recv()

    def y_total(offset):
        part = (x + offset) % 4
        return (
            held[3, part].astype(F32)
            + y_in[0, part].astype(F32)
            + y_in[1, part].astype(F32)
        )

    left = at(z, x - 1, y, core)
    right = at(z, x + 1, y, core)
    held[4, 0] = y_total(2).astype(BF)
    xup = send(held.at[4, 0, 0], x_half.at[0], x_sem, 0, right)
    xdown = send(held.at[4, 0, 1], x_half.at[1], x_sem, 1, left)
    ahead_x = y_total(1)
    behind_x = y_total(3)
    own = y_total(0)
    nearer(1, 0)
    xup.wait_recv()
    held[4, 1, 0] = (ahead_x[0] + x_half[0].astype(F32)).astype(BF)
    held[4, 1, 1] = ahead_x[1].astype(BF)
    xup2 = send(held.at[4, 1], x_in.at[0], x_sem, 2, right)
    xdown.wait_recv()
    held[4, 2, 0] = behind_x[0].astype(BF)
    held[4, 2, 1] = (behind_x[1] + x_half[1].astype(F32)).astype(BF)
    xdown2 = send(held.at[4, 2], x_in.at[1], x_sem, 3, left)
    xup2.wait_recv()
    xdown2.wait_recv()
    held[4, 3] = (own + x_in[0].astype(F32) + x_in[1].astype(F32)).astype(BF)

    zs = []
    for step in (4, 3, 5, 2, 6, 1, 7):
        target = (z + step) % 8
        zs.append(
            send(held.at[4, 3, :, target], z_in.at[step - 1], z_sem, step - 1, around[step - 1])
        )
    go_home(1)
    result = held[4, 3, :, z].astype(F32)
    for copy, step in zip(zs, (4, 3, 5, 2, 6, 1, 7)):
        copy.wait_recv()
        result = result + z_in[step - 1].astype(F32)
    gw_ref[...] = result
    for copy in homes:
        copy.wait_recv()
    rest = swaps + [up, down, up2, down2, xup, xdown, xup2, xdown2] + zs
    for copy in given + homes + rest + list(copies.values()):
        copy.wait_send()


def finish(caps, chunk, number, mate, con, fin, ge, dw):
    total = sum(caps)
    smem = pl.BlockSpec(memory_space=pltpu.SMEM)
    vmem = pl.BlockSpec(memory_space=pltpu.VMEM)
    return pl.pallas_call(
        functools.partial(finish_kernel, caps, chunk),
        in_specs=[smem, smem, smem, vmem, vmem],
        out_specs=[vmem, vmem],
        out_shape=[
            jax.ShapeDtypeStruct((8, 128, 512), BF),
            jax.ShapeDtypeStruct((2, 16, 256), F32),
        ],
        scratch_shapes=[
            pltpu.VMEM((33, 16, 256), BF),
            pltpu.VMEM((33, 16, 256), BF),
            pltpu.VMEM((33, 16, 256), F32),
            pltpu.VMEM((33, 16, 256), F32),
            pltpu.VMEM((2, 2 * total, 16, 256), BF),
            pltpu.VMEM((2 * total + 1, 16, 256), BF),
            pltpu.VMEM((2 * total + 1, 16, 256), BF),
            pltpu.VMEM((2, 8, 8, 16, 256), BF),
            pltpu.VMEM((4, 4, 2, 8, 16, 256), BF),
            pltpu.VMEM((5, 4, 2, 8, 16, 256), BF),
            pltpu.VMEM((2, 2, 2, 8, 16, 256), BF),
            pltpu.VMEM((2, 4, 2, 8, 16, 256), BF),
            pltpu.VMEM((2, 8, 16, 256), BF),
            pltpu.VMEM((2, 2, 8, 16, 256), BF),
            pltpu.VMEM((7, 2, 16, 256), BF),
            pltpu.SemaphoreType.DMA((2, 2, 7)),
            pltpu.SemaphoreType.DMA((2, 2, 2, total // chunk)),
            pltpu.SemaphoreType.DMA((2, 2, 7)),
            pltpu.SemaphoreType.DMA((2, 4)),
            pltpu.SemaphoreType.DMA((2, 4)),
            pltpu.SemaphoreType.DMA((2, 4)),
            pltpu.SemaphoreType.DMA((2, 7)),
        ],
        compiler_params=pltpu.CompilerParams(
            collective_id=number, has_side_effects=True, vmem_limit_bytes=48 * 2**20
        ),
    )(mate, con, fin, ge, dw)


TIGHT = (24, 20, 16, 8)
WIDE = (64, 64, 64, 32)


def plan(ids):
    z, x, y, core = place()
    i32 = jnp.int32
    member_core = jnp.arange(8, dtype=i32)[None, None, :, None] % 2
    block = (ids // 8 % 4 * 2 + member_core) * 8 + ids % 8
    owner_z = ids // 32
    away = (jnp.arange(8, dtype=i32)[None, :, None, None] - owner_z + 8) % 8
    flat = (owner_z * 64 + block).reshape(4, 256)
    is_block = (flat[:, None, :] == jnp.arange(512, dtype=i32)[None, :, None]).astype(BF)
    is_away = (away.reshape(4, 1, 256) == jnp.arange(8, dtype=i32)[None, :, None]).astype(BF)
    wanted = jnp.einsum("ydr,ybr->ydb", is_away, is_block, preferred_element_type=F32) > 0.5
    wanted = wanted.reshape(4, 8, 8, 64)
    team = jnp.arange(64, dtype=i32)
    even = team % 2 == 0

    def far(one, two, three, four):
        return jnp.where(four, 4, jnp.where(three, 3, jnp.where(two, 2, jnp.where(one, 1, 0))))

    up = far(wanted[:, 1], wanted[:, 2], wanted[:, 3], wanted[:, 4] & even)
    down = far(wanted[:, 7], wanted[:, 6], wanted[:, 5], wanted[:, 4] & ~even)
    fars = jnp.stack([up, down], axis=1).astype(i32)
    reach = jnp.arange(1, 5, dtype=i32)[:, None, None, None, None]
    lengths = jnp.sum((fars[None] >= reach).astype(i32), axis=-1)
    fits = jnp.all(lengths <= jnp.array(TIGHT, i32)[:, None, None, None])
    fars = lax.dynamic_index_in_dim(fars, y, 0, keepdims=False)
    fars = lax.dynamic_slice_in_dim(jnp.concatenate([fars, fars], axis=1), z, 8, axis=1)
    key = fars * 64 + 63 - team
    rank = jnp.sum((key[..., :, None] > key[..., None, :]).astype(i32), axis=-2)
    at_rank = rank[..., None, :] == team[:, None]
    order = jnp.sum(jnp.where(at_rank[:, 0], team, 0), axis=-1)

    def mine(a):
        a = lax.dynamic_index_in_dim(a, y, 0, keepdims=False)
        return lax.dynamic_index_in_dim(a, z, 0, keepdims=False).reshape(32)

    my_block, my_away = mine(block), mine(away)
    my_flat = (8 - my_away) % 8 * 64 + my_block
    upwards = (my_away < 4) | ((my_away == 4) & (my_block % 2 == 0))
    hops = jnp.where(upwards, my_away, 8 - my_away)
    hit = my_flat[:, None] == jnp.arange(512, dtype=i32)[None, :]
    ranks = jnp.sum(jnp.where(hit[None], rank.reshape(2, 1, 512), 0), axis=-1)
    spot = jnp.where(upwards, ranks[0], ranks[1])
    refs = jnp.arange(32, dtype=i32)
    first = jnp.min(jnp.where(hit, refs[:, None], 32), axis=0).reshape(8, 64)
    same = my_flat[:, None] == my_flat[None, :]
    earlier = jnp.sum((same[:, None, :] & (refs[None, None, :] < refs[None, :, None])).astype(i32), axis=-1)
    mate = 32 + jnp.sum(
        jnp.where(
            same[:, None, :] & (earlier[:, None, :] == jnp.arange(4, dtype=i32)[None, :, None]),
            refs - 32,
            0,
        ),
        axis=-1,
    )
    firsts = jnp.stack(
        [
            jnp.stack([first[7], first[6], first[5], jnp.where(even, first[4], 32)]),
            jnp.stack([first[1], first[2], first[3], jnp.where(even, 32, first[4])]),
        ]
    )
    at_rank_by_hop = jnp.stack(
        [
            jnp.stack([at_rank[0, 7], at_rank[0, 6], at_rank[0, 5], at_rank[0, 4]]),
            jnp.stack([at_rank[1, 1], at_rank[1, 2], at_rank[1, 3], at_rank[1, 4]]),
        ]
    )
    con = 32 + jnp.sum(jnp.where(at_rank_by_hop, firsts[:, :, None, :] - 32, 0), axis=-1)

    def locate(caps):
        total = sum(caps)
        offset = sum(jnp.where(hops == r + 1, starts(caps)[r], 0) for r in range(4))
        there = jnp.where(upwards, 0, total) + offset + spot
        return jnp.where(my_away == 0, 2 * total + my_block, there)

    def collect(caps):
        total = sum(caps)
        return jnp.stack(
            [
                jnp.where(fars[0, 0] > 0, rank[0, 0], 2 * total),
                jnp.where(fars[1, 0] > 0, total + rank[1, 0], 2 * total),
                first[0],
            ],
            axis=1,
        )

    return fits, order, mate, con, locate, collect


def body(queries, grad_out, enc_states, neighbour_ids, kv_weight):
    row = jnp.pad(neighbour_ids.reshape(1, 4), ((0, 0), (0, 124)))
    pool, ids = spread(row, enc_states[0])
    fits, order, mate, con, locate, collect = plan(ids[:, :, :, 0, :4])
    pool = pool.reshape(64, 16, 256)
    states = lax.cond(
        fits,
        lambda: gather(TIGHT, 4, 2, order, locate(TIGHT), pool, enc_states[0]),
        lambda: gather(WIDE, 16, 3, order, locate(WIDE), pool, enc_states[0]),
    )
    gq, grad_e, dw = attention(states.reshape(512, 512), kv_weight, queries[0], grad_out[0])
    grad_e = grad_e.reshape(4, 128, 512)
    grad_states, grad_weight = lax.cond(
        fits,
        lambda: finish(TIGHT, 4, 4, mate, con, collect(TIGHT), grad_e, dw),
        lambda: finish(WIDE, 16, 5, mate, con, collect(WIDE), grad_e, dw),
    )
    return (gq[None], grad_states[None], grad_weight)


def solution(mesh):
    placed = (
        P("grp", "seq", None),
        P("grp", "seq", None),
        P("grp", "seq", None, None),
        P("grp", "seq", None),
        P(),
    )
    return jax.shard_map(
        body,
        mesh=mesh,
        in_specs=placed,
        out_specs=(P("grp", "seq", None), P("grp", "seq", None, None), P(None, "seq", "grp")),
        check_vma=False,
    )
```

```python
import functools
import math

import jax
import jax.numpy as jnp
from jax import lax
from jax.experimental import pallas as pl
from jax.experimental.pallas import tpu as pltpu
from jax.sharding import PartitionSpec as P

DH = 128
BF = jnp.bfloat16
F32 = jnp.float32
MESH = pl.DeviceIdType.MESH
NT = (((1,), (1,)), ((), ()))
TN = (((0,), (0,)), ((), ()))


def place():
    seq = lax.axis_index("seq")
    grp = lax.axis_index("grp")
    return seq // 4, seq % 4, grp // 2, grp % 2


def at(z, x, y, core):
    return {"seq": (z + 8) % 8 * 4 + (x + 4) % 4, "grp": (y + 4) % 4 * 2 + core}


def teammate(z, y, member):
    return at(z, member // 2, y, member % 2)


def greet(friends):
    barrier = pltpu.get_barrier_semaphore()
    for friend in friends:
        pl.semaphore_signal(barrier, inc=1, device_id=friend, device_id_type=MESH)
    pl.semaphore_wait(barrier, len(friends))


def push(src, dst, send_sem, recv_sem, target):
    copy = pltpu.make_async_remote_copy(
        src_ref=src,
        dst_ref=dst,
        send_sem=send_sem,
        recv_sem=recv_sem,
        device_id=target,
        device_id_type=MESH,
    )
    copy.start()
    return copy


def head_pair(step, y, core):
    return (y + 6 - step // 2) % 4 * 2 + (core + 1 + step % 2) % 2


def attention_kernel(
    states_ref,
    w_ref,
    q_ref,
    go_ref,
    gq_ref,
    ge_ref,
    sums_ref,
    st_ref,
    acc_ref,
    pair_out,
    pair_in,
    far_out,
    y_half,
    core_sem,
    y_sem,
):
    step = pl.program_id(0)
    z, x, y, core = place()
    other = at(z, x, y, 1 - core)
    sides = [at(z, x, y + 1, core), at(z, x, y - 1, core)]
    scale = 1.0 / math.sqrt(DH)

    @pl.when(step == 0)
    def _():
        st_ref[...] = states_ref[...].T
        acc_ref[...] = jnp.zeros_like(acc_ref)
        barrier = pltpu.get_barrier_semaphore()
        for friend in [other] + sides:
            pl.semaphore_signal(barrier, inc=1, device_id=friend, device_id_type=MESH)

    states = states_ref[...]
    wk = w_ref[0]
    wv = w_ref[1]
    keys = jnp.dot(states, wk, preferred_element_type=F32).astype(BF)
    values = jnp.dot(states, wv, preferred_element_type=F32).astype(BF)
    blank = jnp.zeros((64, DH), BF)
    gk_parts = []
    gv_parts = []
    for span in range(2):
        q = q_ref[span * 64 : span * 64 + 64, :]
        go = go_ref[span * 64 : span * 64 + 64, :]
        key = keys[span * 256 : span * 256 + 256, :]
        value = values[span * 256 : span * 256 + 256, :]
        qd = jnp.concatenate(
            [
                jnp.concatenate([q[:, :DH], blank], axis=1),
                jnp.concatenate([blank, q[:, DH:]], axis=1),
            ],
            axis=0,
        )
        gd = jnp.concatenate(
            [
                jnp.concatenate([go[:, :DH], blank], axis=1),
                jnp.concatenate([blank, go[:, DH:]], axis=1),
            ],
            axis=0,
        )
        scores = lax.dot_general(key, qd, NT, preferred_element_type=F32) * scale
        top = jnp.max(scores, axis=0, keepdims=True)
        expo = jnp.exp(scores - top)
        weights = expo / jnp.sum(expo, axis=0, keepdims=True)
        weights_b = weights.astype(BF)
        gp = lax.dot_general(value, gd, NT, preferred_element_type=F32)
        delta = jnp.sum(weights_b.astype(F32) * gp, axis=0, keepdims=True)
        gs = (weights * (gp - delta) * scale).astype(BF)
        gv_parts.append(jnp.dot(weights_b, gd, preferred_element_type=F32).astype(BF))
        gk_parts.append(jnp.dot(gs, qd, preferred_element_type=F32).astype(BF))
        gq = lax.dot_general(gs, key, TN, preferred_element_type=F32).astype(BF)
        gq_ref[span * 64 : span * 64 + 64, :DH] = gq[:64, :DH]
        gq_ref[span * 64 : span * 64 + 64, DH:] = gq[64:, DH:]
    gk = jnp.concatenate(gk_parts, axis=0)
    gv = jnp.concatenate(gv_parts, axis=0)
    total = acc_ref[...]
    total = total + lax.dot_general(gk, wk, NT, preferred_element_type=F32)
    total = total + lax.dot_general(gv, wv, NT, preferred_element_type=F32)
    acc_ref[...] = total

    @pl.when(step == pl.num_programs(0) - 1)
    def _():
        ge_ref[...] = total.astype(BF)

    turned = st_ref[...]
    shares = [jnp.dot(turned, part, preferred_element_type=F32) for part in (gk, gv)]
    slot = step // 2

    def swap(k):
        return pltpu.make_async_remote_copy(
            src_ref=pair_out.at[k],
            dst_ref=pair_in.at[k],
            send_sem=core_sem.at[0, k],
            recv_sem=core_sem.at[1, k],
            device_id=other,
            device_id_type=MESH,
        )

    def opposite(side):
        return pltpu.make_async_remote_copy(
            src_ref=far_out.at[pl.ds(side * 2, 2)],
            dst_ref=y_half.at[side],
            send_sem=y_sem.at[0, side],
            recv_sem=y_sem.at[1, side],
            device_id=sides[side],
            device_id_type=MESH,
        )

    def each(write):
        for kind in range(2):
            for zz in range(8):
                for xx in range(4):
                    row = (zz * 4 + xx) * 16
                    write(xx, kind, zz, shares[kind][row : row + 16, :])

    @pl.when(step % 2 == 0)
    def _():
        def write(xx, kind, zz, part):
            pair_out[slot, xx, kind, zz] = part.astype(BF)

        each(write)

        @pl.when(step == 0)
        def _():
            pl.semaphore_wait(pltpu.get_barrier_semaphore(), 3)

        swap(slot).start()

    @pl.when(step % 2 == 1)
    def _():
        swap(slot).wait_recv()

        @pl.when(step == 1)
        def _():
            def write(xx, kind, zz, part):
                far_out[xx, kind, zz] = (part + pair_in[0, xx, kind, zz].astype(F32)).astype(BF)

            each(write)
            for side in range(2):
                opposite(side).start()

        @pl.when(step > 1)
        def _():
            def write(xx, kind, zz, part):
                sums_ref[slot - 1, xx, kind, zz] = (
                    part + pair_in[slot, xx, kind, zz].astype(F32)
                ).astype(BF)

            each(write)

        @pl.when(step == 7)
        def _():
            opposite(0).wait_recv()
            for part in range(2):
                sums_ref[0, part] = (
                    sums_ref[0, part].astype(F32) + y_half[0, part].astype(F32)
                ).astype(BF)
            opposite(1).wait_recv()
            for part in range(2):
                sums_ref[2, part + 2] = (
                    sums_ref[2, part + 2].astype(F32) + y_half[1, part].astype(F32)
                ).astype(BF)
            for side in range(2):
                opposite(side).wait_send()
            for k in range(4):
                swap(k).wait_send()


def attention(states, weights, queries, grad_out):
    keys, enc = states.shape
    tokens, width = queries.shape

    def columns(i):
        _, _, y, core = place()
        return head_pair(i, y, core)

    return pl.pallas_call(
        attention_kernel,
        grid=(8,),
        in_specs=[
            pl.BlockSpec((keys, enc), lambda i: (0, 0)),
            pl.BlockSpec((2, enc, 256), lambda i: (0, 0, columns(i))),
            pl.BlockSpec((tokens, 256), lambda i: (0, columns(i))),
            pl.BlockSpec((tokens, 256), lambda i: (0, columns(i))),
        ],
        out_specs=[
            pl.BlockSpec((tokens, 256), lambda i: (0, columns(i))),
            pl.BlockSpec((keys, enc), lambda i: (0, 0)),
            pl.BlockSpec((3, 4, 2, 8, 16, 256), lambda i: (0, 0, 0, 0, 0, 0)),
        ],
        out_shape=[
            jax.ShapeDtypeStruct((tokens, width), BF),
            jax.ShapeDtypeStruct((keys, enc), BF),
            jax.ShapeDtypeStruct((3, 4, 2, 8, 16, 256), BF),
        ],
        scratch_shapes=[
            pltpu.VMEM((enc, keys), BF),
            pltpu.VMEM((keys, enc), F32),
            pltpu.VMEM((4, 4, 2, 8, 16, 256), BF),
            pltpu.VMEM((4, 4, 2, 8, 16, 256), BF),
            pltpu.VMEM((4, 2, 8, 16, 256), BF),
            pltpu.VMEM((2, 2, 2, 8, 16, 256), BF),
            pltpu.SemaphoreType.DMA((2, 4)),
            pltpu.SemaphoreType.DMA((2, 2)),
        ],
        compiler_params=pltpu.CompilerParams(
            collective_id=6, has_side_effects=True, vmem_limit_bytes=60 * 2**20
        ),
        cost_estimate=pl.CostEstimate(
            flops=7_200_000_000, bytes_accessed=12_000_000, transcendentals=600_000
        ),
    )(states, weights, queries, grad_out)


OUT = ((0, 256), (256, 128), (384, 128))
BACK = ((0, 128), (128, 256), (384, 128))


def piece(member):
    return pl.ds(pl.multiple_of(member * 16, 16), 16)


def spread_kernel(
    mine_ref, enc_ref, pool_ref, packed_ref, ids_ref, team_sem, xy_sem, zc_sem, own_sem
):
    z, x, y, core = place()
    me = x * 2 + core
    columns = pl.ds(*OUT[0])
    team = [teammate(z, y, (me + k) % 8) for k in range(1, 8)]
    flat = [at(z, x + k // 4, y + k % 4, core) for k in range(1, 16)]
    upright = [at(z + k // 2, x, y, (core + k % 2) % 2) for k in range(1, 16)]
    own = pltpu.make_async_copy(enc_ref.at[:, piece(me), columns], pool_ref.at[me], own_sem)
    own.start()
    lane = lax.broadcasted_iota(jnp.int32, (1, 128), 1) - (z % 4 * 32 + me * 4)
    line = jnp.zeros((1, 128), jnp.int32)
    for ref in range(4):
        line = jnp.where(lane == ref, mine_ref[0, ref // 2, ref % 2], line)
    ids_ref[z, core, x, y] = line
    greet(flat + upright + [at(z, x + k, y, 1 - core) for k in range(1, 4)])
    rows = []
    for k in range(1, 16):
        rows.append(
            push(
                ids_ref.at[z, core, x, y],
                ids_ref.at[z, core, x, y],
                xy_sem.at[0, k - 1],
                xy_sem.at[1, k - 1],
                flat[k - 1],
            )
        )
    pieces = []
    for k in range(1, 8):
        pieces.append(
            push(
                enc_ref.at[:, piece((me + k) % 8), columns],
                pool_ref.at[me],
                team_sem.at[0, k - 1],
                team_sem.at[1, k - 1],
                team[k - 1],
            )
        )
    for copy in rows:
        copy.wait_recv()
    planes = []
    for k in range(1, 16):
        planes.append(
            push(
                ids_ref.at[z, core],
                ids_ref.at[z, core],
                zc_sem.at[0, k - 1],
                zc_sem.at[1, k - 1],
                upright[k - 1],
            )
        )
    own.wait()
    for copy in planes + pieces:
        copy.wait_recv()
    for yy in range(4):
        for half in range(2):
            line = jnp.zeros((1, 128), jnp.int32)
            for zz in range(half * 4, half * 4 + 4):
                for cc in range(2):
                    for xx in range(4):
                        line = line + ids_ref[zz, cc, xx, yy]
            packed_ref[yy, half : half + 1, :] = line
    for copy in rows + pieces + planes:
        copy.wait_send()


def spread(mine, enc):
    return pl.pallas_call(
        spread_kernel,
        in_specs=[
            pl.BlockSpec(memory_space=pltpu.SMEM),
            pl.BlockSpec(memory_space=pl.ANY),
        ],
        out_specs=[
            pl.BlockSpec(memory_space=pltpu.VMEM),
            pl.BlockSpec(memory_space=pltpu.VMEM),
        ],
        out_shape=[
            jax.ShapeDtypeStruct((8, 8, 16, OUT[0][1]), BF),
            jax.ShapeDtypeStruct((4, 2, 128), jnp.int32),
        ],
        scratch_shapes=[
            pltpu.VMEM((8, 2, 4, 4, 1, 128), jnp.int32),
            pltpu.SemaphoreType.DMA((2, 7)),
            pltpu.SemaphoreType.DMA((2, 15)),
            pltpu.SemaphoreType.DMA((2, 15)),
            pltpu.SemaphoreType.DMA,
        ],
        compiler_params=pltpu.CompilerParams(
            collective_id=1, has_side_effects=True, vmem_limit_bytes=60 * 2**20
        ),
    )(mine, enc)


def starts(caps):
    return [0] + [sum(caps[: r + 1]) for r in range(len(caps))]


def chunks(marks, cap):
    ends = [mark for mark in marks if mark <= cap]
    return list(zip([0] + ends[:-1], ends))


def gather_kernel(caps, order_ref, loc_ref, pool_ref, enc_ref, states_ref, *scratch):
    count = len(OUT)
    pools = (pool_ref,) + scratch[: count - 1]
    packeds = scratch[count - 1 : 2 * count - 1]
    arrs = scratch[2 * count - 1 : 3 * count - 1]
    stages = scratch[3 * count - 1 : 4 * count - 1]
    ring_sem, team_sem, spread_sem, own_sem = scratch[4 * count - 1 :]
    z, x, y, core = place()
    me = x * 2 + core
    total = sum(caps)
    first = starts(caps)
    marks = sorted(set(caps))
    friends = [teammate(z, y, (me + k) % 8) for k in range(1, 8)]
    ahead = at(z + 1, x, y, core)
    behind = at(z - 1, x, y, core)
    owns = []
    for h in range(1, count):
        owns.append(
            pltpu.make_async_copy(
                enc_ref.at[:, piece(me), pl.ds(*OUT[h])], pools[h].at[me], own_sem.at[h - 1]
            )
        )
        owns[-1].start()
    greet(friends + [ahead, behind])
    copies = {}

    def forward(h, d, r, i, src, low, high):
        copies[h, d, r, i] = push(
            src,
            arrs[h].at[pl.ds(d * total + first[r] + low, high - low)],
            ring_sem.at[0, h, d, r, i],
            ring_sem.at[1, h, d, r, i],
            ahead if d == 0 else behind,
        )

    def first_hop(h):
        pool = pools[h]
        for i, (low, high) in enumerate(chunks(marks, caps[0])):
            for d in range(2):

                def fill(j, carry, d=d):
                    block = order_ref[d, j]
                    packeds[h][d, j] = pool[block // 8, block % 8]
                    return carry

                lax.fori_loop(low, high, fill, 0, unroll=2)
                forward(h, d, 0, i, packeds[h].at[d, pl.ds(low, high - low)], low, high)

        def keep(j, carry):
            for k in range(8):
                arrs[h][2 * total + j * 8 + k] = pool[j, k]
            return carry

        lax.fori_loop(0, 8, keep, 0)

    def next_hop(h, r):
        for i, (low, high) in enumerate(chunks(marks, caps[r])):
            for d in range(2):
                copies[h, d, r - 1, i].wait_recv()
                src = arrs[h].at[pl.ds(d * total + first[r - 1] + low, high - low)]
                forward(h, d, r, i, src, low, high)

    hands = []

    def hand_out(h):
        for r in range(4):
            done = len(chunks(marks, caps[r + 1])) if r < 3 else 0
            for i in range(done, len(chunks(marks, caps[r]))):
                for d in range(2):
                    copies[h, d, r, i].wait_recv()

        def pick(i, carry):
            for k in range(4):
                stages[h][i, k] = arrs[h][loc_ref[i * 4 + k]]
            return carry

        lax.fori_loop(0, 8, pick, 0)
        for k in range(1, 8):
            hands.append(
                push(
                    stages[h].at[(me + k) % 8],
                    states_ref.at[:, piece(me), pl.ds(*OUT[h])],
                    team_sem.at[0, h, k - 1],
                    team_sem.at[1, h, k - 1],
                    friends[k - 1],
                )
            )
        low, wide = OUT[h]
        states_ref[:, piece(me), low : low + wide] = stages[h][me]

    pieces = {}

    def more(h):
        for k in range(1, 8):
            pieces[h, k] = push(
                enc_ref.at[:, piece((me + k) % 8), pl.ds(*OUT[h])],
                pools[h].at[me],
                spread_sem.at[0, h - 1, k - 1],
                spread_sem.at[1, h - 1, k - 1],
                friends[k - 1],
            )

    def here(h):
        owns[h - 1].wait()
        for k in range(1, 8):
            pieces[h, k].wait_recv()

    more(1)
    more(2)
    first_hop(0)
    here(1)
    first_hop(1)
    next_hop(0, 1)
    here(2)
    first_hop(2)
    next_hop(1, 1)
    next_hop(0, 2)
    next_hop(2, 1)
    next_hop(1, 2)
    next_hop(0, 3)
    next_hop(2, 2)
    next_hop(1, 3)
    hand_out(0)
    next_hop(2, 3)
    hand_out(1)
    hand_out(2)
    for copy in hands:
        copy.wait_recv()
    for copy in hands + list(pieces.values()) + list(copies.values()):
        copy.wait_send()


def gather(caps, number, order, loc, pool, enc):
    total = sum(caps)
    count = len(OUT)
    return pl.pallas_call(
        functools.partial(gather_kernel, caps),
        in_specs=[
            pl.BlockSpec(memory_space=pltpu.SMEM),
            pl.BlockSpec(memory_space=pltpu.SMEM),
            pl.BlockSpec(memory_space=pltpu.VMEM),
            pl.BlockSpec(memory_space=pl.ANY),
        ],
        out_specs=pl.BlockSpec(memory_space=pltpu.VMEM),
        out_shape=jax.ShapeDtypeStruct((4, 128, 512), BF),
        scratch_shapes=[pltpu.VMEM((8, 8, 16, wide), BF) for _, wide in OUT[1:]]
        + [pltpu.VMEM((2, caps[0], 16, wide), BF) for _, wide in OUT]
        + [pltpu.VMEM((2 * total + 64, 16, wide), BF) for _, wide in OUT]
        + [pltpu.VMEM((8, 4, 16, wide), BF) for _, wide in OUT]
        + [
            pltpu.SemaphoreType.DMA((2, count, 2, 4, 4)),
            pltpu.SemaphoreType.DMA((2, count, 7)),
            pltpu.SemaphoreType.DMA((2, count - 1, 7)),
            pltpu.SemaphoreType.DMA((count - 1,)),
        ],
        compiler_params=pltpu.CompilerParams(
            collective_id=number, has_side_effects=True, vmem_limit_bytes=60 * 2**20
        ),
    )(order, loc, pool, enc)


def finish_kernel(
    caps,
    mate_ref,
    con_ref,
    fin_ref,
    ge_ref,
    sums_ref,
    gs_ref,
    gw_ref,
    *scratch,
):
    count = len(BACK)
    takens, combs, outbs, inbs, dones = (scratch[k * count : k * count + count] for k in range(5))
    held, y_in, x_half, x_in, z_in, team_sem, ring_sem, home_sem, y_sem, x_sem, z_sem = scratch[
        5 * count :
    ]
    z, x, y, core = place()
    me = x * 2 + core
    total = sum(caps)
    first = starts(caps)
    marks = sorted(set(caps))
    friends = [teammate(z, y, (me + k) % 8) for k in range(1, 8)]
    around = [at(z + k, x, y, core) for k in range(1, 8)]
    ahead = around[0]
    behind = around[6]
    sides = [at(z, x, y + 1, core), at(z, x, y - 1, core)]
    greet(friends + around + sides)

    def send(src, dst, sems, slot, target):
        return push(src, dst, sems.at[0, slot], sems.at[1, slot], target)

    given = []

    def give(h):
        for k in range(1, 8):
            given.append(
                push(
                    ge_ref.at[:, piece((me + k) % 8), pl.ds(*BACK[h])],
                    takens[h].at[pl.ds(me * 4, 4)],
                    team_sem.at[0, h, k - 1],
                    team_sem.at[1, h, k - 1],
                    friends[k - 1],
                )
            )

    give(0)
    up = send(sums_ref.at[0], y_in.at[0], y_sem, 0, sides[0])
    down = send(sums_ref.at[2], y_in.at[1], y_sem, 1, sides[1])
    give(1)
    give(2)

    def combine(h):
        taken, comb = takens[h], combs[h]
        low, wide = BACK[h]
        taken[pl.ds(me * 4, 4)] = ge_ref[:, piece(me), low : low + wide]
        taken[32] = jnp.zeros((16, wide), BF)
        comb[32] = jnp.zeros((16, wide), F32)
        inbs[h][2 * total] = jnp.zeros((16, wide), BF)
        for copy in given[h * 7 : h * 7 + 7]:
            copy.wait_recv()

        def step(i, carry):
            row = taken[mate_ref[0, i]].astype(F32)
            for t in range(1, 4):
                row = row + taken[mate_ref[t, i]].astype(F32)
            comb[i] = row
            return carry

        lax.fori_loop(0, 32, step, 0, unroll=4)

    copies = {}

    def back(h, r, i, added):
        comb, inb, outb = combs[h], inbs[h], outbs[h]
        low, high = chunks(marks, caps[r])[i]
        for d in range(2):
            base = d * total + first[r]
            if added:
                copies[h, d, r + 1, i].wait_recv()
                further = d * total + first[r + 1]

                def fill(j, carry, d=d, base=base, further=further):
                    outb[base + j] = (
                        comb[con_ref[d, r, j]] + inb[further + j].astype(F32)
                    ).astype(BF)
                    return carry
            else:

                def fill(j, carry, d=d, base=base):
                    outb[base + j] = comb[con_ref[d, r, j]].astype(BF)
                    return carry

            lax.fori_loop(low, high, fill, 0, unroll=2)
            copies[h, d, r, i] = push(
                outb.at[pl.ds(base + low, high - low)],
                inb.at[pl.ds(base + low, high - low)],
                ring_sem.at[0, h, d, r, i],
                ring_sem.at[1, h, d, r, i],
                behind if d == 0 else ahead,
            )

    def farthest(h):
        for i in range(len(chunks(marks, caps[3]))):
            back(h, 3, i, False)
        for r in (2, 1, 0):
            for i in range(len(chunks(marks, caps[r + 1])), len(chunks(marks, caps[r]))):
                back(h, r, i, False)

    def nearer(h, r):
        for i in range(len(chunks(marks, caps[r + 1]))):
            back(h, r, i, True)

    homes = []

    def go_home(h):
        comb, inb = combs[h], inbs[h]
        for i in range(len(chunks(marks, caps[0]))):
            for d in range(2):
                copies[h, d, 0, i].wait_recv()

        def close(i, carry):
            for k in range(8):
                b = i * 8 + k
                dones[h][i, k] = (
                    inb[fin_ref[0, b]].astype(F32)
                    + inb[fin_ref[1, b]].astype(F32)
                    + comb[fin_ref[2, b]]
                ).astype(BF)
            return carry

        lax.fori_loop(0, 8, close, 0)
        for k in range(1, 8):
            homes.append(
                push(
                    dones[h].at[(me + k) % 8],
                    gs_ref.at[:, piece(me), pl.ds(*BACK[h])],
                    home_sem.at[0, h, k - 1],
                    home_sem.at[1, h, k - 1],
                    friends[k - 1],
                )
            )
        low, wide = BACK[h]
        gs_ref[:, piece(me), low : low + wide] = dones[h][me]

    def y_total(offset):
        part = (x + offset) % 4
        return (
            sums_ref[1, part].astype(F32)
            + y_in[0, part].astype(F32)
            + y_in[1, part].astype(F32)
        )

    combine(0)
    farthest(0)
    combine(1)
    nearer(0, 2)
    farthest(1)
    nearer(0, 1)
    combine(2)
    nearer(1, 2)
    nearer(0, 0)
    farthest(2)
    left = at(z, x - 1, y, core)
    right = at(z, x + 1, y, core)
    up.wait_recv()
    down.wait_recv()
    held[0] = y_total(2).astype(BF)
    xup = send(held.at[0, 0], x_half.at[0], x_sem, 0, right)
    xdown = send(held.at[0, 1], x_half.at[1], x_sem, 1, left)
    nearer(1, 1)
    ahead_x = y_total(1)
    xup.wait_recv()
    held[1, 0] = (ahead_x[0] + x_half[0].astype(F32)).astype(BF)
    held[1, 1] = ahead_x[1].astype(BF)
    xup2 = send(held.at[1], x_in.at[0], x_sem, 2, right)
    behind_x = y_total(3)
    xdown.wait_recv()
    held[2, 0] = behind_x[0].astype(BF)
    held[2, 1] = (behind_x[1] + x_half[1].astype(F32)).astype(BF)
    xdown2 = send(held.at[2], x_in.at[1], x_sem, 3, left)
    go_home(0)
    nearer(2, 2)
    nearer(1, 0)
    xup2.wait_recv()
    xdown2.wait_recv()
    held[3] = (y_total(0) + x_in[0].astype(F32) + x_in[1].astype(F32)).astype(BF)
    zs = []
    for step in (4, 3, 5, 2, 6, 1, 7):
        target = (z + step) % 8
        zs.append(
            send(held.at[3, :, target], z_in.at[step - 1], z_sem, step - 1, around[step - 1])
        )
    nearer(2, 1)
    go_home(1)
    nearer(2, 0)
    go_home(2)
    result = held[3, :, z].astype(F32)
    for copy, step in zip(zs, (4, 3, 5, 2, 6, 1, 7)):
        copy.wait_recv()
        result = result + z_in[step - 1].astype(F32)
    gw_ref[...] = result
    for copy in homes:
        copy.wait_recv()
    rest = [up, down, xup, xdown, xup2, xdown2] + zs
    for copy in given + homes + rest + list(copies.values()):
        copy.wait_send()


def finish(caps, number, mate, con, fin, ge, sums):
    total = sum(caps)
    count = len(BACK)
    smem = pl.BlockSpec(memory_space=pltpu.SMEM)
    vmem = pl.BlockSpec(memory_space=pltpu.VMEM)
    return pl.pallas_call(
        functools.partial(finish_kernel, caps),
        in_specs=[smem, smem, smem, vmem, vmem],
        out_specs=[vmem, vmem],
        out_shape=[
            jax.ShapeDtypeStruct((8, 128, 512), BF),
            jax.ShapeDtypeStruct((2, 16, 256), F32),
        ],
        scratch_shapes=[pltpu.VMEM((33, 16, wide), BF) for _, wide in BACK]
        + [pltpu.VMEM((33, 16, wide), F32) for _, wide in BACK]
        + [pltpu.VMEM((2 * total, 16, wide), BF) for _, wide in BACK]
        + [pltpu.VMEM((2 * total + 1, 16, wide), BF) for _, wide in BACK]
        + [pltpu.VMEM((8, 8, 16, wide), BF) for _, wide in BACK]
        + [
            pltpu.VMEM((4, 2, 8, 16, 256), BF),
            pltpu.VMEM((2, 4, 2, 8, 16, 256), BF),
            pltpu.VMEM((2, 8, 16, 256), BF),
            pltpu.VMEM((2, 2, 8, 16, 256), BF),
            pltpu.VMEM((7, 2, 16, 256), BF),
            pltpu.SemaphoreType.DMA((2, count, 7)),
            pltpu.SemaphoreType.DMA((2, count, 2, 4, 4)),
            pltpu.SemaphoreType.DMA((2, count, 7)),
            pltpu.SemaphoreType.DMA((2, 2)),
            pltpu.SemaphoreType.DMA((2, 4)),
            pltpu.SemaphoreType.DMA((2, 7)),
        ],
        compiler_params=pltpu.CompilerParams(
            collective_id=number, has_side_effects=True, vmem_limit_bytes=48 * 2**20
        ),
    )(mate, con, fin, ge, sums)


TIGHT = (22, 18, 14, 6)
MIDDLE = (24, 20, 16, 8)
WIDE = (64, 64, 64, 32)
CAPS = (TIGHT, MIDDLE, WIDE)


def plan(ids):
    z, x, y, core = place()
    i32 = jnp.int32
    place_of = jnp.arange(256, dtype=i32)[None, :]
    block = (ids // 8 % 4 * 2 + place_of // 4 % 2) * 8 + ids % 8
    owner_z = ids // 32
    away = (place_of // 32 - owner_z + 8) % 8
    flat = owner_z * 64 + block
    is_block = (flat[:, None, :] == jnp.arange(512, dtype=i32)[None, :, None]).astype(BF)
    is_away = (away[:, None, :] == jnp.arange(8, dtype=i32)[None, :, None]).astype(BF)
    wanted = jnp.einsum("ydr,ybr->ydb", is_away, is_block, preferred_element_type=F32) > 0.5
    wanted = wanted.reshape(4, 8, 8, 64)
    team = jnp.arange(64, dtype=i32)
    even = team % 2 == 0

    def far(one, two, three, four):
        return jnp.where(four, 4, jnp.where(three, 3, jnp.where(two, 2, jnp.where(one, 1, 0))))

    up = far(wanted[:, 1], wanted[:, 2], wanted[:, 3], wanted[:, 4] & even)
    down = far(wanted[:, 7], wanted[:, 6], wanted[:, 5], wanted[:, 4] & ~even)
    fars = jnp.stack([up, down], axis=1).astype(i32)
    reach = jnp.arange(1, 5, dtype=i32)[:, None, None, None, None]
    lengths = jnp.sum((fars[None] >= reach).astype(i32), axis=-1)
    longest = jnp.max(lengths, axis=(1, 2, 3))
    level = jnp.where(
        jnp.all(longest <= jnp.array(TIGHT, i32)),
        0,
        jnp.where(jnp.all(longest <= jnp.array(MIDDLE, i32)), 1, 2),
    )
    fars = lax.dynamic_index_in_dim(fars, y, 0, keepdims=False)
    fars = lax.dynamic_slice_in_dim(jnp.concatenate([fars, fars], axis=1), z, 8, axis=1)
    key = fars * 64 + 63 - team
    rank = jnp.sum((key[..., :, None] > key[..., None, :]).astype(i32), axis=-2)
    at_rank = rank[..., :, None] == team
    order = jnp.sum(jnp.where(at_rank[:, 0], team[:, None], 0), axis=-2)

    def mine(a):
        return lax.dynamic_slice(a, (y, z * 32), (1, 32)).reshape(32)

    my_block, my_away = mine(block), mine(away)
    my_flat = (8 - my_away) % 8 * 64 + my_block
    upwards = (my_away < 4) | ((my_away == 4) & (my_block % 2 == 0))
    hops = jnp.where(upwards, my_away, 8 - my_away)
    hit = my_flat[:, None] == jnp.arange(512, dtype=i32)[None, :]
    ranks = lax.dot_general(
        rank.reshape(2, 512).astype(BF), hit.astype(BF), NT, preferred_element_type=F32
    ).astype(i32)
    spot = jnp.where(upwards, ranks[0], ranks[1])
    refs = jnp.arange(32, dtype=i32)
    first = jnp.min(jnp.where(hit, refs[:, None], 32), axis=0).reshape(8, 64)
    same = my_flat[:, None] == my_flat[None, :]
    earlier = jnp.sum(
        (same[None] & (refs[None, :, None] < refs[:, None, None])).astype(i32), axis=1
    )
    turns = jnp.arange(4, dtype=i32)[:, None, None]
    mate = 32 + jnp.sum(
        jnp.where(same[None] & (earlier[None] == turns), refs[:, None] - 32, 0), axis=1
    )
    firsts = jnp.stack(
        [
            jnp.stack([first[7], first[6], first[5], jnp.where(even, first[4], 32)]),
            jnp.stack([first[1], first[2], first[3], jnp.where(even, 32, first[4])]),
        ]
    )
    at_rank_by_hop = jnp.stack(
        [
            jnp.stack([at_rank[0, 7], at_rank[0, 6], at_rank[0, 5], at_rank[0, 4]]),
            jnp.stack([at_rank[1, 1], at_rank[1, 2], at_rank[1, 3], at_rank[1, 4]]),
        ]
    )
    con = 32 + jnp.sum(jnp.where(at_rank_by_hop, firsts[..., None] - 32, 0), axis=-2)

    def locate(caps):
        total = sum(caps)
        offset = sum(jnp.where(hops == r + 1, starts(caps)[r], 0) for r in range(4))
        there = jnp.where(upwards, 0, total) + offset + spot
        return jnp.where(my_away == 0, 2 * total + my_block, there)

    def collect(caps):
        total = sum(caps)
        return jnp.stack(
            [
                jnp.where(fars[0, 0] > 0, rank[0, 0], 2 * total),
                jnp.where(fars[1, 0] > 0, total + rank[1, 0], 2 * total),
                first[0],
            ]
        )

    return level, order, mate, con, locate, collect


def body(queries, grad_out, enc_states, neighbour_ids, kv_weight):
    enc = enc_states[0]
    pool, ids = spread(neighbour_ids, enc)
    level, order, mate, con, locate, collect = plan(ids.reshape(4, 256))
    states = lax.switch(
        level,
        [
            lambda caps=caps, number=number: gather(caps, number, order, locate(caps), pool, enc)
            for caps, number in zip(CAPS, (2, 3, 7))
        ],
    )
    gq, grad_e, sums = attention(states.reshape(512, 512), kv_weight, queries[0], grad_out[0])
    grad_e = grad_e.reshape(4, 128, 512)
    grad_states, grad_weight = lax.switch(
        level,
        [
            lambda caps=caps, number=number: finish(
                caps, number, mate, con, collect(caps), grad_e, sums
            )
            for caps, number in zip(CAPS, (4, 5, 8))
        ],
    )
    return (gq[None], grad_states[None], grad_weight)


def solution(mesh):
    placed = (
        P("grp", "seq", None),
        P("grp", "seq", None),
        P("grp", "seq", None, None),
        P("grp", "seq", None),
        P(),
    )
    return jax.shard_map(
        body,
        mesh=mesh,
        in_specs=placed,
        out_specs=(P("grp", "seq", None), P("grp", "seq", None, None), P(None, "seq", "grp")),
        check_vma=False,
    )
```

```python
import functools
import math

import jax
import jax.numpy as jnp
from jax import lax
from jax.experimental import pallas as pl
from jax.experimental.pallas import tpu as pltpu
from jax.sharding import PartitionSpec as P

DH = 128
BF = jnp.bfloat16
F32 = jnp.float32
MESH = pl.DeviceIdType.MESH
NT = (((1,), (1,)), ((), ()))
TN = (((0,), (0,)), ((), ()))


def place():
    seq = lax.axis_index("seq")
    grp = lax.axis_index("grp")
    return seq // 4, seq % 4, grp // 2, grp % 2


def at(z, x, y, core):
    return {"seq": (z + 8) % 8 * 4 + (x + 4) % 4, "grp": (y + 4) % 4 * 2 + core}


def teammate(z, y, member):
    return at(z, member // 2, y, member % 2)


def greet(friends):
    barrier = pltpu.get_barrier_semaphore()
    for friend in friends:
        pl.semaphore_signal(barrier, inc=1, device_id=friend, device_id_type=MESH)
    pl.semaphore_wait(barrier, len(friends))


def push(src, dst, send_sem, recv_sem, target):
    copy = pltpu.make_async_remote_copy(
        src_ref=src,
        dst_ref=dst,
        send_sem=send_sem,
        recv_sem=recv_sem,
        device_id=target,
        device_id_type=MESH,
    )
    copy.start()
    return copy


def head_pair(step, y, core):
    return (y + 6 - step // 2) % 4 * 2 + (core + 1 + step % 2) % 2


def attention_kernel(
    states_ref,
    w_ref,
    q_ref,
    go_ref,
    gq_ref,
    ge_ref,
    sums_ref,
    st_ref,
    acc_ref,
    pair_out,
    pair_in,
    far_out,
    y_half,
    core_sem,
    y_sem,
):
    step = pl.program_id(0)
    z, x, y, core = place()
    other = at(z, x, y, 1 - core)
    sides = [at(z, x, y + 1, core), at(z, x, y - 1, core)]
    scale = 1.0 / math.sqrt(DH)

    @pl.when(step == 0)
    def _():
        st_ref[...] = states_ref[...].T
        acc_ref[...] = jnp.zeros_like(acc_ref)
        barrier = pltpu.get_barrier_semaphore()
        for friend in [other] + sides:
            pl.semaphore_signal(barrier, inc=1, device_id=friend, device_id_type=MESH)

    states = states_ref[...]
    wk = w_ref[0]
    wv = w_ref[1]
    keys = jnp.dot(states, wk, preferred_element_type=F32).astype(BF)
    values = jnp.dot(states, wv, preferred_element_type=F32).astype(BF)
    blank = jnp.zeros((64, DH), BF)
    gk_parts = []
    gv_parts = []
    ahead = []
    for span in range(2):
        q = q_ref[span * 64 : span * 64 + 64, :]
        go = go_ref[span * 64 : span * 64 + 64, :]
        key = keys[span * 256 : span * 256 + 256, :]
        value = values[span * 256 : span * 256 + 256, :]
        qd = jnp.concatenate(
            [
                jnp.concatenate([q[:, :DH], blank], axis=1),
                jnp.concatenate([blank, q[:, DH:]], axis=1),
            ],
            axis=0,
        )
        gd = jnp.concatenate(
            [
                jnp.concatenate([go[:, :DH], blank], axis=1),
                jnp.concatenate([blank, go[:, DH:]], axis=1),
            ],
            axis=0,
        )
        scores = lax.dot_general(key, qd, NT, preferred_element_type=F32) * scale
        gp = lax.dot_general(value, gd, NT, preferred_element_type=F32)
        ahead.append((key, qd, gd, scores, gp))
    middle = []
    for key, qd, gd, scores, gp in ahead:
        top = jnp.max(scores, axis=0, keepdims=True)
        expo = jnp.exp(scores - top)
        weights = expo / jnp.sum(expo, axis=0, keepdims=True)
        weights_b = weights.astype(BF)
        delta = jnp.sum(weights_b.astype(F32) * gp, axis=0, keepdims=True)
        gs = (weights * (gp - delta) * scale).astype(BF)
        middle.append((key, qd, gd, weights_b, gs))
    for span, (key, qd, gd, weights_b, gs) in enumerate(middle):
        gv_parts.append(jnp.dot(weights_b, gd, preferred_element_type=F32).astype(BF))
        gk_parts.append(jnp.dot(gs, qd, preferred_element_type=F32).astype(BF))
        gq = lax.dot_general(gs, key, TN, preferred_element_type=F32).astype(BF)
        gq_ref[span * 64 : span * 64 + 64, :DH] = gq[:64, :DH]
        gq_ref[span * 64 : span * 64 + 64, DH:] = gq[64:, DH:]
    gk = jnp.concatenate(gk_parts, axis=0)
    gv = jnp.concatenate(gv_parts, axis=0)
    total = acc_ref[...]
    total = total + lax.dot_general(gk, wk, NT, preferred_element_type=F32)
    total = total + lax.dot_general(gv, wv, NT, preferred_element_type=F32)
    acc_ref[...] = total

    @pl.when(step == pl.num_programs(0) - 1)
    def _():
        ge_ref[...] = total.astype(BF)

    turned = st_ref[...]
    shares = [jnp.dot(turned, part, preferred_element_type=F32) for part in (gk, gv)]
    slot = step // 2

    def swap(k):
        return pltpu.make_async_remote_copy(
            src_ref=pair_out.at[k],
            dst_ref=pair_in.at[k],
            send_sem=core_sem.at[0, k],
            recv_sem=core_sem.at[1, k],
            device_id=other,
            device_id_type=MESH,
        )

    def opposite(side):
        return pltpu.make_async_remote_copy(
            src_ref=far_out.at[pl.ds(side * 2, 2)],
            dst_ref=y_half.at[side],
            send_sem=y_sem.at[0, side],
            recv_sem=y_sem.at[1, side],
            device_id=sides[side],
            device_id_type=MESH,
        )

    def each(write):
        for kind in range(2):
            for zz in range(8):
                for xx in range(4):
                    row = (zz * 4 + xx) * 16
                    write(xx, kind, zz, shares[kind][row : row + 16, :])

    @pl.when(step % 2 == 0)
    def _():
        def write(xx, kind, zz, part):
            pair_out[slot, xx, kind, zz] = part.astype(BF)

        each(write)

        @pl.when(step == 0)
        def _():
            pl.semaphore_wait(pltpu.get_barrier_semaphore(), 3)

        swap(slot).start()

    @pl.when(step % 2 == 1)
    def _():
        swap(slot).wait_recv()

        @pl.when(step == 1)
        def _():
            def write(xx, kind, zz, part):
                far_out[xx, kind, zz] = (part + pair_in[0, xx, kind, zz].astype(F32)).astype(BF)

            each(write)
            for side in range(2):
                opposite(side).start()

        @pl.when(step > 1)
        def _():
            def write(xx, kind, zz, part):
                sums_ref[slot - 1, xx, kind, zz] = (
                    part + pair_in[slot, xx, kind, zz].astype(F32)
                ).astype(BF)

            each(write)

        @pl.when(step == 7)
        def _():
            opposite(0).wait_recv()
            for part in range(2):
                sums_ref[0, part] = (
                    sums_ref[0, part].astype(F32) + y_half[0, part].astype(F32)
                ).astype(BF)
            opposite(1).wait_recv()
            for part in range(2):
                sums_ref[2, part + 2] = (
                    sums_ref[2, part + 2].astype(F32) + y_half[1, part].astype(F32)
                ).astype(BF)
            for side in range(2):
                opposite(side).wait_send()
            for k in range(4):
                swap(k).wait_send()


def attention(states, weights, queries, grad_out):
    keys, enc = states.shape
    tokens, width = queries.shape

    def columns(i):
        _, _, y, core = place()
        return head_pair(i, y, core)

    return pl.pallas_call(
        attention_kernel,
        grid=(8,),
        in_specs=[
            pl.BlockSpec((keys, enc), lambda i: (0, 0)),
            pl.BlockSpec((2, enc, 256), lambda i: (0, 0, columns(i))),
            pl.BlockSpec((tokens, 256), lambda i: (0, columns(i))),
            pl.BlockSpec((tokens, 256), lambda i: (0, columns(i))),
        ],
        out_specs=[
            pl.BlockSpec((tokens, 256), lambda i: (0, columns(i))),
            pl.BlockSpec((keys, enc), lambda i: (0, 0)),
            pl.BlockSpec((3, 4, 2, 8, 16, 256), lambda i: (0, 0, 0, 0, 0, 0)),
        ],
        out_shape=[
            jax.ShapeDtypeStruct((tokens, width), BF),
            jax.ShapeDtypeStruct((keys, enc), BF),
            jax.ShapeDtypeStruct((3, 4, 2, 8, 16, 256), BF),
        ],
        scratch_shapes=[
            pltpu.VMEM((enc, keys), BF),
            pltpu.VMEM((keys, enc), F32),
            pltpu.VMEM((4, 4, 2, 8, 16, 256), BF),
            pltpu.VMEM((4, 4, 2, 8, 16, 256), BF),
            pltpu.VMEM((4, 2, 8, 16, 256), BF),
            pltpu.VMEM((2, 2, 2, 8, 16, 256), BF),
            pltpu.SemaphoreType.DMA((2, 4)),
            pltpu.SemaphoreType.DMA((2, 2)),
        ],
        compiler_params=pltpu.CompilerParams(
            collective_id=6, has_side_effects=True, vmem_limit_bytes=60 * 2**20
        ),
        cost_estimate=pl.CostEstimate(
            flops=7_200_000_000, bytes_accessed=12_000_000, transcendentals=600_000
        ),
    )(states, weights, queries, grad_out)


OUT = ((0, 256), (256, 128), (384, 128))
BACK = ((0, 128), (128, 256), (384, 128))
EARLY = 2


def piece(member):
    return pl.ds(pl.multiple_of(member * 16, 16), 16)


def spread_kernel(mine_ref, enc_ref, *rest):
    pool_refs = rest[:EARLY]
    packed_ref, ids_ref, team_sem, xy_sem, zc_sem, own_sem = rest[EARLY:]
    z, x, y, core = place()
    me = x * 2 + core
    team = [teammate(z, y, (me + k) % 8) for k in range(1, 8)]
    flat = [at(z, x + k // 4, y + k % 4, core) for k in range(1, 16)]
    upright = [at(z + k // 2, x, y, (core + k % 2) % 2) for k in range(1, 16)]
    owns = []
    for h in range(EARLY):
        owns.append(
            pltpu.make_async_copy(
                enc_ref.at[:, piece(me), pl.ds(*OUT[h])], pool_refs[h].at[me], own_sem.at[h]
            )
        )
        owns[h].start()
    lane = lax.broadcasted_iota(jnp.int32, (1, 128), 1) - (z % 4 * 32 + me * 4)
    line = jnp.zeros((1, 128), jnp.int32)
    for ref in range(4):
        line = jnp.where(lane == ref, mine_ref[0, ref // 2, ref % 2], line)
    ids_ref[z, core, x, y] = line
    greet(flat + upright + [at(z, x + k, y, 1 - core) for k in range(1, 4)])
    rows = []
    for k in range(1, 16):
        rows.append(
            push(
                ids_ref.at[z, core, x, y],
                ids_ref.at[z, core, x, y],
                xy_sem.at[0, k - 1],
                xy_sem.at[1, k - 1],
                flat[k - 1],
            )
        )
    pieces = []

    def hand(h):
        for k in range(1, 8):
            pieces.append(
                push(
                    enc_ref.at[:, piece((me + k) % 8), pl.ds(*OUT[h])],
                    pool_refs[h].at[me],
                    team_sem.at[0, h, k - 1],
                    team_sem.at[1, h, k - 1],
                    team[k - 1],
                )
            )

    hand(0)
    for copy in rows:
        copy.wait_recv()
    planes = []
    for k in range(1, 16):
        planes.append(
            push(
                ids_ref.at[z, core],
                ids_ref.at[z, core],
                zc_sem.at[0, k - 1],
                zc_sem.at[1, k - 1],
                upright[k - 1],
            )
        )
    for h in range(1, EARLY):
        hand(h)
    for copy in owns:
        copy.wait()
    for copy in planes + pieces:
        copy.wait_recv()
    for yy in range(4):
        for half in range(2):
            line = jnp.zeros((1, 128), jnp.int32)
            for zz in range(half * 4, half * 4 + 4):
                for cc in range(2):
                    for xx in range(4):
                        line = line + ids_ref[zz, cc, xx, yy]
            packed_ref[yy, half : half + 1, :] = line
    for copy in rows + pieces + planes:
        copy.wait_send()


def spread(mine, enc):
    return pl.pallas_call(
        spread_kernel,
        in_specs=[
            pl.BlockSpec(memory_space=pltpu.SMEM),
            pl.BlockSpec(memory_space=pl.ANY),
        ],
        out_specs=[pl.BlockSpec(memory_space=pltpu.VMEM)] * (EARLY + 1),
        out_shape=[jax.ShapeDtypeStruct((8, 8, 16, wide), BF) for _, wide in OUT[:EARLY]]
        + [jax.ShapeDtypeStruct((4, 2, 128), jnp.int32)],
        scratch_shapes=[
            pltpu.VMEM((8, 2, 4, 4, 1, 128), jnp.int32),
            pltpu.SemaphoreType.DMA((2, EARLY, 7)),
            pltpu.SemaphoreType.DMA((2, 15)),
            pltpu.SemaphoreType.DMA((2, 15)),
            pltpu.SemaphoreType.DMA((EARLY,)),
        ],
        compiler_params=pltpu.CompilerParams(
            collective_id=1, has_side_effects=True, vmem_limit_bytes=60 * 2**20
        ),
    )(mine, enc)


def starts(caps):
    return [0] + [sum(caps[: r + 1]) for r in range(len(caps))]


def chunks(marks, cap):
    ends = [mark for mark in marks if mark <= cap]
    return list(zip([0] + ends[:-1], ends))


def gather_kernel(caps, order_ref, loc_ref, *rest):
    count = len(OUT)
    late = count - EARLY
    enc_ref, states_ref = rest[EARLY : EARLY + 2]
    pools = rest[:EARLY] + rest[EARLY + 2 : EARLY + 2 + late]
    scratch = rest[EARLY + 2 + late :]
    packeds, arrs, stages = (scratch[k * count : k * count + count] for k in range(3))
    ring_sem, team_sem, spread_sem, own_sem = scratch[3 * count :]
    z, x, y, core = place()
    me = x * 2 + core
    total = sum(caps)
    first = starts(caps)
    marks = sorted(set(caps))
    friends = [teammate(z, y, (me + k) % 8) for k in range(1, 8)]
    ahead = at(z + 1, x, y, core)
    behind = at(z - 1, x, y, core)
    owns = []
    for h in range(EARLY, count):
        owns.append(
            pltpu.make_async_copy(
                enc_ref.at[:, piece(me), pl.ds(*OUT[h])], pools[h].at[me], own_sem.at[h - EARLY]
            )
        )
        owns[-1].start()
    greet(friends + [ahead, behind])
    copies = {}

    def forward(h, d, r, i, src, low, high):
        copies[h, d, r, i] = push(
            src,
            arrs[h].at[pl.ds(d * total + first[r] + low, high - low)],
            ring_sem.at[0, h, d, r, i],
            ring_sem.at[1, h, d, r, i],
            ahead if d == 0 else behind,
        )

    def first_hop(h):
        pool = pools[h]
        for i, (low, high) in enumerate(chunks(marks, caps[0])):
            for d in range(2):

                def fill(j, carry, d=d):
                    block = order_ref[d, j]
                    packeds[h][d, j] = pool[block // 8, block % 8]
                    return carry

                lax.fori_loop(low, high, fill, 0, unroll=2)
                forward(h, d, 0, i, packeds[h].at[d, pl.ds(low, high - low)], low, high)

        def keep(j, carry):
            for k in range(8):
                arrs[h][2 * total + j * 8 + k] = pool[j, k]
            return carry

        lax.fori_loop(0, 8, keep, 0)

    def next_hop(h, r):
        for i, (low, high) in enumerate(chunks(marks, caps[r])):
            for d in range(2):
                copies[h, d, r - 1, i].wait_recv()
                src = arrs[h].at[pl.ds(d * total + first[r - 1] + low, high - low)]
                forward(h, d, r, i, src, low, high)

    hands = []

    def hand_out(h):
        for r in range(4):
            done = len(chunks(marks, caps[r + 1])) if r < 3 else 0
            for i in range(done, len(chunks(marks, caps[r]))):
                for d in range(2):
                    copies[h, d, r, i].wait_recv()

        def pick(i, carry):
            for k in range(4):
                stages[h][i, k] = arrs[h][loc_ref[i * 4 + k]]
            return carry

        lax.fori_loop(0, 8, pick, 0)
        for k in range(1, 8):
            hands.append(
                push(
                    stages[h].at[(me + k) % 8],
                    states_ref.at[:, piece(me), pl.ds(*OUT[h])],
                    team_sem.at[0, h, k - 1],
                    team_sem.at[1, h, k - 1],
                    friends[k - 1],
                )
            )
        low, wide = OUT[h]
        states_ref[:, piece(me), low : low + wide] = stages[h][me]

    pieces = {}

    def more(h):
        for k in range(1, 8):
            pieces[h, k] = push(
                enc_ref.at[:, piece((me + k) % 8), pl.ds(*OUT[h])],
                pools[h].at[me],
                spread_sem.at[0, h - EARLY, k - 1],
                spread_sem.at[1, h - EARLY, k - 1],
                friends[k - 1],
            )

    def here(h):
        if h < EARLY:
            return
        owns[h - EARLY].wait()
        for k in range(1, 8):
            pieces[h, k].wait_recv()

    for h in range(EARLY, count):
        more(h)
    first_hop(0)
    here(1)
    first_hop(1)
    next_hop(0, 1)
    here(2)
    first_hop(2)
    next_hop(1, 1)
    next_hop(0, 2)
    next_hop(2, 1)
    next_hop(1, 2)
    next_hop(0, 3)
    next_hop(2, 2)
    next_hop(1, 3)
    hand_out(0)
    next_hop(2, 3)
    hand_out(1)
    hand_out(2)
    for copy in hands:
        copy.wait_recv()
    for copy in hands + list(pieces.values()) + list(copies.values()):
        copy.wait_send()


def gather(caps, number, order, loc, pools, enc):
    total = sum(caps)
    count = len(OUT)
    return pl.pallas_call(
        functools.partial(gather_kernel, caps),
        in_specs=[pl.BlockSpec(memory_space=pltpu.SMEM)] * 2
        + [pl.BlockSpec(memory_space=pltpu.VMEM)] * EARLY
        + [pl.BlockSpec(memory_space=pl.ANY)],
        out_specs=pl.BlockSpec(memory_space=pltpu.VMEM),
        out_shape=jax.ShapeDtypeStruct((4, 128, 512), BF),
        scratch_shapes=[pltpu.VMEM((8, 8, 16, wide), BF) for _, wide in OUT[EARLY:]]
        + [pltpu.VMEM((2, caps[0], 16, wide), BF) for _, wide in OUT]
        + [pltpu.VMEM((2 * total + 64, 16, wide), BF) for _, wide in OUT]
        + [pltpu.VMEM((8, 4, 16, wide), BF) for _, wide in OUT]
        + [
            pltpu.SemaphoreType.DMA((2, count, 2, 4, 4)),
            pltpu.SemaphoreType.DMA((2, count, 7)),
            pltpu.SemaphoreType.DMA((2, count - EARLY, 7)),
            pltpu.SemaphoreType.DMA((count - EARLY,)),
        ],
        compiler_params=pltpu.CompilerParams(
            collective_id=number, has_side_effects=True, vmem_limit_bytes=60 * 2**20
        ),
    )(order, loc, *pools, enc)


def finish_kernel(
    caps,
    mate_ref,
    con_ref,
    fin_ref,
    ge_ref,
    sums_ref,
    gs_ref,
    gw_ref,
    *scratch,
):
    count = len(BACK)
    takens, combs, outbs, inbs, dones = (scratch[k * count : k * count + count] for k in range(5))
    held, y_in, x_half, x_in, z_in, team_sem, ring_sem, home_sem, y_sem, x_sem, z_sem = scratch[
        5 * count :
    ]
    z, x, y, core = place()
    me = x * 2 + core
    total = sum(caps)
    first = starts(caps)
    marks = sorted(set(caps))
    friends = [teammate(z, y, (me + k) % 8) for k in range(1, 8)]
    around = [at(z + k, x, y, core) for k in range(1, 8)]
    ahead = around[0]
    behind = around[6]
    sides = [at(z, x, y + 1, core), at(z, x, y - 1, core)]
    greet(friends + around + sides)

    def send(src, dst, sems, slot, target):
        return push(src, dst, sems.at[0, slot], sems.at[1, slot], target)

    given = []

    def give(h):
        for k in range(1, 8):
            given.append(
                push(
                    ge_ref.at[:, piece((me + k) % 8), pl.ds(*BACK[h])],
                    takens[h].at[pl.ds(me * 4, 4)],
                    team_sem.at[0, h, k - 1],
                    team_sem.at[1, h, k - 1],
                    friends[k - 1],
                )
            )

    give(0)
    up = send(sums_ref.at[0], y_in.at[0], y_sem, 0, sides[0])
    down = send(sums_ref.at[2], y_in.at[1], y_sem, 1, sides[1])
    give(1)
    give(2)

    def combine(h):
        taken, comb = takens[h], combs[h]
        low, wide = BACK[h]
        taken[pl.ds(me * 4, 4)] = ge_ref[:, piece(me), low : low + wide]
        taken[32] = jnp.zeros((16, wide), BF)
        comb[32] = jnp.zeros((16, wide), F32)
        inbs[h][2 * total] = jnp.zeros((16, wide), BF)
        for copy in given[h * 7 : h * 7 + 7]:
            copy.wait_recv()

        def step(i, carry):
            row = taken[mate_ref[0, i]].astype(F32)
            for t in range(1, 4):
                row = row + taken[mate_ref[t, i]].astype(F32)
            comb[i] = row
            return carry

        lax.fori_loop(0, 32, step, 0, unroll=4)

    copies = {}

    def back(h, r, i, added):
        comb, inb, outb = combs[h], inbs[h], outbs[h]
        low, high = chunks(marks, caps[r])[i]
        for d in range(2):
            base = d * total + first[r]
            if added:
                copies[h, d, r + 1, i].wait_recv()
                further = d * total + first[r + 1]

                def fill(j, carry, d=d, base=base, further=further):
                    outb[base + j] = (
                        comb[con_ref[d, r, j]] + inb[further + j].astype(F32)
                    ).astype(BF)
                    return carry
            else:

                def fill(j, carry, d=d, base=base):
                    outb[base + j] = comb[con_ref[d, r, j]].astype(BF)
                    return carry

            lax.fori_loop(low, high, fill, 0, unroll=2)
            copies[h, d, r, i] = push(
                outb.at[pl.ds(base + low, high - low)],
                inb.at[pl.ds(base + low, high - low)],
                ring_sem.at[0, h, d, r, i],
                ring_sem.at[1, h, d, r, i],
                behind if d == 0 else ahead,
            )

    def farthest(h):
        for i in range(len(chunks(marks, caps[3]))):
            back(h, 3, i, False)
        for r in (2, 1, 0):
            for i in range(len(chunks(marks, caps[r + 1])), len(chunks(marks, caps[r]))):
                back(h, r, i, False)

    def nearer(h, r):
        for i in range(len(chunks(marks, caps[r + 1]))):
            back(h, r, i, True)

    homes = []

    def go_home(h):
        comb, inb = combs[h], inbs[h]
        for i in range(len(chunks(marks, caps[0]))):
            for d in range(2):
                copies[h, d, 0, i].wait_recv()

        def close(i, carry):
            for k in range(8):
                b = i * 8 + k
                dones[h][i, k] = (
                    inb[fin_ref[0, b]].astype(F32)
                    + inb[fin_ref[1, b]].astype(F32)
                    + comb[fin_ref[2, b]]
                ).astype(BF)
            return carry

        lax.fori_loop(0, 8, close, 0)
        for k in range(1, 8):
            homes.append(
                push(
                    dones[h].at[(me + k) % 8],
                    gs_ref.at[:, piece(me), pl.ds(*BACK[h])],
                    home_sem.at[0, h, k - 1],
                    home_sem.at[1, h, k - 1],
                    friends[k - 1],
                )
            )
        low, wide = BACK[h]
        gs_ref[:, piece(me), low : low + wide] = dones[h][me]

    def y_total(offset):
        part = (x + offset) % 4
        return (
            sums_ref[1, part].astype(F32)
            + y_in[0, part].astype(F32)
            + y_in[1, part].astype(F32)
        )

    combine(0)
    farthest(0)
    combine(1)
    nearer(0, 2)
    farthest(1)
    nearer(0, 1)
    combine(2)
    nearer(1, 2)
    nearer(0, 0)
    farthest(2)
    left = at(z, x - 1, y, core)
    right = at(z, x + 1, y, core)
    up.wait_recv()
    down.wait_recv()
    held[0] = y_total(2).astype(BF)
    xup = send(held.at[0, 0], x_half.at[0], x_sem, 0, right)
    xdown = send(held.at[0, 1], x_half.at[1], x_sem, 1, left)
    nearer(1, 1)
    ahead_x = y_total(1)
    xup.wait_recv()
    held[1, 0] = (ahead_x[0] + x_half[0].astype(F32)).astype(BF)
    held[1, 1] = ahead_x[1].astype(BF)
    xup2 = send(held.at[1], x_in.at[0], x_sem, 2, right)
    behind_x = y_total(3)
    xdown.wait_recv()
    held[2, 0] = behind_x[0].astype(BF)
    held[2, 1] = (behind_x[1] + x_half[1].astype(F32)).astype(BF)
    xdown2 = send(held.at[2], x_in.at[1], x_sem, 3, left)
    go_home(0)
    nearer(2, 2)
    nearer(1, 0)
    xup2.wait_recv()
    xdown2.wait_recv()
    held[3] = (y_total(0) + x_in[0].astype(F32) + x_in[1].astype(F32)).astype(BF)
    zs = []
    for step in (4, 3, 5, 2, 6, 1, 7):
        target = (z + step) % 8
        zs.append(
            send(held.at[3, :, target], z_in.at[step - 1], z_sem, step - 1, around[step - 1])
        )
    nearer(2, 1)
    go_home(1)
    nearer(2, 0)
    go_home(2)
    result = held[3, :, z].astype(F32)
    for copy, step in zip(zs, (4, 3, 5, 2, 6, 1, 7)):
        copy.wait_recv()
        result = result + z_in[step - 1].astype(F32)
    gw_ref[...] = result
    for copy in homes:
        copy.wait_recv()
    rest = [up, down, xup, xdown, xup2, xdown2] + zs
    for copy in given + homes + rest + list(copies.values()):
        copy.wait_send()


def finish(caps, number, mate, con, fin, ge, sums):
    total = sum(caps)
    count = len(BACK)
    smem = pl.BlockSpec(memory_space=pltpu.SMEM)
    vmem = pl.BlockSpec(memory_space=pltpu.VMEM)
    return pl.pallas_call(
        functools.partial(finish_kernel, caps),
        in_specs=[smem, smem, smem, vmem, vmem],
        out_specs=[vmem, vmem],
        out_shape=[
            jax.ShapeDtypeStruct((8, 128, 512), BF),
            jax.ShapeDtypeStruct((2, 16, 256), F32),
        ],
        scratch_shapes=[pltpu.VMEM((33, 16, wide), BF) for _, wide in BACK]
        + [pltpu.VMEM((33, 16, wide), F32) for _, wide in BACK]
        + [pltpu.VMEM((2 * total, 16, wide), BF) for _, wide in BACK]
        + [pltpu.VMEM((2 * total + 1, 16, wide), BF) for _, wide in BACK]
        + [pltpu.VMEM((8, 8, 16, wide), BF) for _, wide in BACK]
        + [
            pltpu.VMEM((4, 2, 8, 16, 256), BF),
            pltpu.VMEM((2, 4, 2, 8, 16, 256), BF),
            pltpu.VMEM((2, 8, 16, 256), BF),
            pltpu.VMEM((2, 2, 8, 16, 256), BF),
            pltpu.VMEM((7, 2, 16, 256), BF),
            pltpu.SemaphoreType.DMA((2, count, 7)),
            pltpu.SemaphoreType.DMA((2, count, 2, 4, 4)),
            pltpu.SemaphoreType.DMA((2, count, 7)),
            pltpu.SemaphoreType.DMA((2, 2)),
            pltpu.SemaphoreType.DMA((2, 4)),
            pltpu.SemaphoreType.DMA((2, 7)),
        ],
        compiler_params=pltpu.CompilerParams(
            collective_id=number, has_side_effects=True, vmem_limit_bytes=48 * 2**20
        ),
    )(mate, con, fin, ge, sums)


TIGHT = (22, 18, 14, 6)
MIDDLE = (24, 20, 16, 8)
WIDE = (64, 64, 64, 32)
CAPS = (TIGHT, MIDDLE, WIDE)


def plan(ids):
    z, x, y, core = place()
    i32 = jnp.int32
    place_of = jnp.arange(256, dtype=i32)[None, :]
    block = (ids // 8 % 4 * 2 + place_of // 4 % 2) * 8 + ids % 8
    owner_z = ids // 32
    away = (place_of // 32 - owner_z + 8) % 8
    flat = owner_z * 64 + block
    is_block = (flat[:, None, :] == jnp.arange(512, dtype=i32)[None, :, None]).astype(BF)
    is_away = (away[:, None, :] == jnp.arange(8, dtype=i32)[None, :, None]).astype(BF)
    wanted = jnp.einsum("ydr,ybr->ydb", is_away, is_block, preferred_element_type=F32) > 0.5
    wanted = wanted.reshape(4, 8, 8, 64)
    team = jnp.arange(64, dtype=i32)
    even = team % 2 == 0

    def far(one, two, three, four):
        return jnp.where(four, 4, jnp.where(three, 3, jnp.where(two, 2, jnp.where(one, 1, 0))))

    up = far(wanted[:, 1], wanted[:, 2], wanted[:, 3], wanted[:, 4] & even)
    down = far(wanted[:, 7], wanted[:, 6], wanted[:, 5], wanted[:, 4] & ~even)
    fars = jnp.stack([up, down], axis=1).astype(i32)
    reach = jnp.arange(1, 5, dtype=i32)[:, None, None, None, None]
    lengths = jnp.sum((fars[None] >= reach).astype(i32), axis=-1)
    longest = jnp.max(lengths, axis=(1, 2, 3))
    level = jnp.where(
        jnp.all(longest <= jnp.array(TIGHT, i32)),
        0,
        jnp.where(jnp.all(longest <= jnp.array(MIDDLE, i32)), 1, 2),
    )
    fars = lax.dynamic_index_in_dim(fars, y, 0, keepdims=False)
    fars = lax.dynamic_slice_in_dim(jnp.concatenate([fars, fars], axis=1), z, 8, axis=1)
    key = fars * 64 + 63 - team
    rank = jnp.sum((key[..., :, None] > key[..., None, :]).astype(i32), axis=-2)
    at_rank = rank[..., :, None] == team
    order = jnp.sum(jnp.where(at_rank[:, 0], team[:, None], 0), axis=-2)

    def mine(a):
        return lax.dynamic_slice(a, (y, z * 32), (1, 32)).reshape(32)

    my_block, my_away = mine(block), mine(away)
    my_flat = (8 - my_away) % 8 * 64 + my_block
    upwards = (my_away < 4) | ((my_away == 4) & (my_block % 2 == 0))
    hops = jnp.where(upwards, my_away, 8 - my_away)
    hit = my_flat[:, None] == jnp.arange(512, dtype=i32)[None, :]
    ranks = lax.dot_general(
        rank.reshape(2, 512).astype(BF), hit.astype(BF), NT, preferred_element_type=F32
    ).astype(i32)
    spot = jnp.where(upwards, ranks[0], ranks[1])
    refs = jnp.arange(32, dtype=i32)
    first = jnp.min(jnp.where(hit, refs[:, None], 32), axis=0).reshape(8, 64)
    same = my_flat[:, None] == my_flat[None, :]
    earlier = jnp.sum(
        (same[None] & (refs[None, :, None] < refs[:, None, None])).astype(i32), axis=1
    )
    turns = jnp.arange(4, dtype=i32)[:, None, None]
    mate = 32 + jnp.sum(
        jnp.where(same[None] & (earlier[None] == turns), refs[:, None] - 32, 0), axis=1
    )
    firsts = jnp.stack(
        [
            jnp.stack([first[7], first[6], first[5], jnp.where(even, first[4], 32)]),
            jnp.stack([first[1], first[2], first[3], jnp.where(even, 32, first[4])]),
        ]
    )
    at_rank_by_hop = jnp.stack(
        [
            jnp.stack([at_rank[0, 7], at_rank[0, 6], at_rank[0, 5], at_rank[0, 4]]),
            jnp.stack([at_rank[1, 1], at_rank[1, 2], at_rank[1, 3], at_rank[1, 4]]),
        ]
    )
    con = 32 + jnp.sum(jnp.where(at_rank_by_hop, firsts[..., None] - 32, 0), axis=-2)

    def locate(caps):
        total = sum(caps)
        offset = sum(jnp.where(hops == r + 1, starts(caps)[r], 0) for r in range(4))
        there = jnp.where(upwards, 0, total) + offset + spot
        return jnp.where(my_away == 0, 2 * total + my_block, there)

    def collect(caps):
        total = sum(caps)
        return jnp.stack(
            [
                jnp.where(fars[0, 0] > 0, rank[0, 0], 2 * total),
                jnp.where(fars[1, 0] > 0, total + rank[1, 0], 2 * total),
                first[0],
            ]
        )

    return level, order, mate, con, locate, collect


def body(queries, grad_out, enc_states, neighbour_ids, kv_weight):
    enc = enc_states[0]
    *pools, ids = spread(neighbour_ids, enc)
    level, order, mate, con, locate, collect = plan(ids.reshape(4, 256))
    states = lax.switch(
        level,
        [
            lambda caps=caps, number=number: gather(caps, number, order, locate(caps), pools, enc)
            for caps, number in zip(CAPS, (2, 3, 7))
        ],
    )
    gq, grad_e, sums = attention(states.reshape(512, 512), kv_weight, queries[0], grad_out[0])
    grad_e = grad_e.reshape(4, 128, 512)
    grad_states, grad_weight = lax.switch(
        level,
        [
            lambda caps=caps, number=number: finish(
                caps, number, mate, con, collect(caps), grad_e, sums
            )
            for caps, number in zip(CAPS, (4, 5, 8))
        ],
    )
    return (gq[None], grad_states[None], grad_weight)


def solution(mesh):
    placed = (
        P("grp", "seq", None),
        P("grp", "seq", None),
        P("grp", "seq", None, None),
        P("grp", "seq", None),
        P(),
    )
    return jax.shard_map(
        body,
        mesh=mesh,
        in_specs=placed,
        out_specs=(P("grp", "seq", None), P("grp", "seq", None, None), P(None, "seq", "grp")),
        check_vma=False,
    )
```

```python
import functools
import math

import jax
import jax.numpy as jnp
from jax import lax
from jax.experimental import pallas as pl
from jax.experimental.pallas import tpu as pltpu
from jax.sharding import PartitionSpec as P

DH = 128
BF = jnp.bfloat16
F32 = jnp.float32
MESH = pl.DeviceIdType.MESH
NT = (((1,), (1,)), ((), ()))
TN = (((0,), (0,)), ((), ()))


def place():
    seq = lax.axis_index("seq")
    grp = lax.axis_index("grp")
    return seq // 4, seq % 4, grp // 2, grp % 2


def at(z, x, y, core):
    return {"seq": (z + 8) % 8 * 4 + (x + 4) % 4, "grp": (y + 4) % 4 * 2 + core}


def teammate(z, y, member):
    return at(z, member // 2, y, member % 2)


def greet(friends):
    barrier = pltpu.get_barrier_semaphore()
    for friend in friends:
        pl.semaphore_signal(barrier, inc=1, device_id=friend, device_id_type=MESH)
    pl.semaphore_wait(barrier, len(friends))


def push(src, dst, send_sem, recv_sem, target):
    copy = pltpu.make_async_remote_copy(
        src_ref=src,
        dst_ref=dst,
        send_sem=send_sem,
        recv_sem=recv_sem,
        device_id=target,
        device_id_type=MESH,
    )
    copy.start()
    return copy


def head_pair(step, y, core):
    return (y + 6 - step // 2) % 4 * 2 + (core + 1 + step % 2) % 2


def attention_kernel(
    states_ref,
    w_ref,
    next_ref,
    q_ref,
    go_ref,
    gq_ref,
    ge_ref,
    sums_ref,
    st_ref,
    acc_ref,
    now_ref,
    later_ref,
    pair_out,
    pair_in,
    far_out,
    y_half,
    core_sem,
    y_sem,
):
    step = pl.program_id(0)
    z, x, y, core = place()
    other = at(z, x, y, 1 - core)
    sides = [at(z, x, y + 1, core), at(z, x, y - 1, core)]
    scale = 1.0 / math.sqrt(DH)

    @pl.when(step == 0)
    def _():
        st_ref[...] = states_ref[...].T
        acc_ref[...] = jnp.zeros_like(acc_ref)
        for kind in range(2):
            later_ref[kind] = jnp.dot(
                states_ref[...], w_ref[kind], preferred_element_type=F32
            ).astype(BF)
        barrier = pltpu.get_barrier_semaphore()
        for friend in [other] + sides:
            pl.semaphore_signal(barrier, inc=1, device_id=friend, device_id_type=MESH)

    states = states_ref[...]
    wk = w_ref[0]
    wv = w_ref[1]
    now_ref[...] = later_ref[...]
    keys = now_ref[0]
    values = now_ref[1]
    blank = jnp.zeros((64, DH), BF)
    gk_parts = []
    gv_parts = []
    ahead = []
    for span in range(2):
        q = q_ref[span * 64 : span * 64 + 64, :]
        go = go_ref[span * 64 : span * 64 + 64, :]
        key = keys[span * 256 : span * 256 + 256, :]
        value = values[span * 256 : span * 256 + 256, :]
        qd = jnp.concatenate(
            [
                jnp.concatenate([q[:, :DH], blank], axis=1),
                jnp.concatenate([blank, q[:, DH:]], axis=1),
            ],
            axis=0,
        )
        gd = jnp.concatenate(
            [
                jnp.concatenate([go[:, :DH], blank], axis=1),
                jnp.concatenate([blank, go[:, DH:]], axis=1),
            ],
            axis=0,
        )
        scores = lax.dot_general(key, qd, NT, preferred_element_type=F32) * scale
        gp = lax.dot_general(value, gd, NT, preferred_element_type=F32)
        ahead.append((key, qd, gd, scores, gp))
    middle = []
    for kind in range(2):
        later_ref[kind] = jnp.dot(states, next_ref[kind], preferred_element_type=F32).astype(BF)
    for key, qd, gd, scores, gp in ahead:
        top = jnp.max(scores, axis=0, keepdims=True)
        expo = jnp.exp(scores - top)
        weights = expo / jnp.sum(expo, axis=0, keepdims=True)
        weights_b = weights.astype(BF)
        delta = jnp.sum(weights_b.astype(F32) * gp, axis=0, keepdims=True)
        gs = (weights * (gp - delta) * scale).astype(BF)
        middle.append((key, qd, gd, weights_b, gs))
    for span, (key, qd, gd, weights_b, gs) in enumerate(middle):
        gv_parts.append(jnp.dot(weights_b, gd, preferred_element_type=F32).astype(BF))
        gk_parts.append(jnp.dot(gs, qd, preferred_element_type=F32).astype(BF))
        gq = lax.dot_general(gs, key, TN, preferred_element_type=F32).astype(BF)
        gq_ref[span * 64 : span * 64 + 64, :DH] = gq[:64, :DH]
        gq_ref[span * 64 : span * 64 + 64, DH:] = gq[64:, DH:]
    gk = jnp.concatenate(gk_parts, axis=0)
    gv = jnp.concatenate(gv_parts, axis=0)
    total = acc_ref[...]
    total = total + lax.dot_general(
        jnp.concatenate([gk, gv], axis=1),
        jnp.concatenate([wk, wv], axis=1),
        NT,
        preferred_element_type=F32,
    )
    acc_ref[...] = total

    @pl.when(step == pl.num_programs(0) - 1)
    def _():
        ge_ref[...] = total.astype(BF)

    turned = st_ref[...]
    shares = [jnp.dot(turned, part, preferred_element_type=F32) for part in (gk, gv)]
    slot = step // 2

    def swap(k):
        return pltpu.make_async_remote_copy(
            src_ref=pair_out.at[k],
            dst_ref=pair_in.at[k],
            send_sem=core_sem.at[0, k],
            recv_sem=core_sem.at[1, k],
            device_id=other,
            device_id_type=MESH,
        )

    def opposite(side):
        return pltpu.make_async_remote_copy(
            src_ref=far_out.at[pl.ds(side * 2, 2)],
            dst_ref=y_half.at[side],
            send_sem=y_sem.at[0, side],
            recv_sem=y_sem.at[1, side],
            device_id=sides[side],
            device_id_type=MESH,
        )

    def each(write):
        for kind in range(2):
            for zz in range(8):
                for xx in range(4):
                    row = (zz * 4 + xx) * 16
                    write(xx, kind, zz, shares[kind][row : row + 16, :])

    @pl.when(step % 2 == 0)
    def _():
        def write(xx, kind, zz, part):
            pair_out[slot, xx, kind, zz] = part.astype(BF)

        each(write)

        @pl.when(step == 0)
        def _():
            pl.semaphore_wait(pltpu.get_barrier_semaphore(), 3)

        swap(slot).start()

    @pl.when(step % 2 == 1)
    def _():
        swap(slot).wait_recv()

        @pl.when(step == 1)
        def _():
            def write(xx, kind, zz, part):
                far_out[xx, kind, zz] = (part + pair_in[0, xx, kind, zz].astype(F32)).astype(BF)

            each(write)
            for side in range(2):
                opposite(side).start()

        @pl.when(step > 1)
        def _():
            def write(xx, kind, zz, part):
                sums_ref[slot - 1, xx, kind, zz] = (
                    part + pair_in[slot, xx, kind, zz].astype(F32)
                ).astype(BF)

            each(write)

        @pl.when(step == 7)
        def _():
            opposite(0).wait_recv()
            for part in range(2):
                sums_ref[0, part] = (
                    sums_ref[0, part].astype(F32) + y_half[0, part].astype(F32)
                ).astype(BF)
            opposite(1).wait_recv()
            for part in range(2):
                sums_ref[2, part + 2] = (
                    sums_ref[2, part + 2].astype(F32) + y_half[1, part].astype(F32)
                ).astype(BF)
            for side in range(2):
                opposite(side).wait_send()
            for k in range(4):
                swap(k).wait_send()


def attention(states, weights, queries, grad_out):
    keys, enc = states.shape
    tokens, width = queries.shape

    def columns(i):
        _, _, y, core = place()
        return head_pair(i, y, core)

    return pl.pallas_call(
        attention_kernel,
        grid=(8,),
        in_specs=[
            pl.BlockSpec((keys, enc), lambda i: (0, 0)),
            pl.BlockSpec((2, enc, 256), lambda i: (0, 0, columns(i))),
            pl.BlockSpec((2, enc, 256), lambda i: (0, 0, columns((i + 1) % 8))),
            pl.BlockSpec((tokens, 256), lambda i: (0, columns(i))),
            pl.BlockSpec((tokens, 256), lambda i: (0, columns(i))),
        ],
        out_specs=[
            pl.BlockSpec((tokens, 256), lambda i: (0, columns(i))),
            pl.BlockSpec((keys, enc), lambda i: (0, 0)),
            pl.BlockSpec((3, 4, 2, 8, 16, 256), lambda i: (0, 0, 0, 0, 0, 0)),
        ],
        out_shape=[
            jax.ShapeDtypeStruct((tokens, width), BF),
            jax.ShapeDtypeStruct((keys, enc), BF),
            jax.ShapeDtypeStruct((3, 4, 2, 8, 16, 256), BF),
        ],
        scratch_shapes=[
            pltpu.VMEM((enc, keys), BF),
            pltpu.VMEM((keys, enc), F32),
            pltpu.VMEM((2, keys, 256), BF),
            pltpu.VMEM((2, keys, 256), BF),
            pltpu.VMEM((4, 4, 2, 8, 16, 256), BF),
            pltpu.VMEM((4, 4, 2, 8, 16, 256), BF),
            pltpu.VMEM((4, 2, 8, 16, 256), BF),
            pltpu.VMEM((2, 2, 2, 8, 16, 256), BF),
            pltpu.SemaphoreType.DMA((2, 4)),
            pltpu.SemaphoreType.DMA((2, 2)),
        ],
        compiler_params=pltpu.CompilerParams(
            collective_id=6, has_side_effects=True, vmem_limit_bytes=60 * 2**20
        ),
        cost_estimate=pl.CostEstimate(
            flops=7_200_000_000, bytes_accessed=12_000_000, transcendentals=600_000
        ),
    )(states, weights, weights, queries, grad_out)


OUT = ((0, 256), (256, 128), (384, 128))
BACK = ((0, 128), (128, 256), (384, 128))
EARLY = 2


def piece(member):
    return pl.ds(pl.multiple_of(member * 16, 16), 16)


def spread_kernel(mine_ref, enc_ref, *rest):
    pool_refs = rest[:EARLY]
    packed_ref, ids_ref, team_sem, xy_sem, zc_sem, own_sem = rest[EARLY:]
    z, x, y, core = place()
    me = x * 2 + core
    team = [teammate(z, y, (me + k) % 8) for k in range(1, 8)]
    flat = [at(z, x + k // 4, y + k % 4, core) for k in range(1, 16)]
    upright = [at(z + k // 2, x, y, (core + k % 2) % 2) for k in range(1, 16)]
    owns = []
    for h in range(EARLY):
        owns.append(
            pltpu.make_async_copy(
                enc_ref.at[:, piece(me), pl.ds(*OUT[h])], pool_refs[h].at[me], own_sem.at[h]
            )
        )
        owns[h].start()
    lane = lax.broadcasted_iota(jnp.int32, (1, 128), 1) - (z % 4 * 32 + me * 4)
    line = jnp.zeros((1, 128), jnp.int32)
    for ref in range(4):
        line = jnp.where(lane == ref, mine_ref[0, ref // 2, ref % 2], line)
    ids_ref[z, core, x, y] = line
    greet(flat + upright + [at(z, x + k, y, 1 - core) for k in range(1, 4)])
    rows = []
    for k in range(1, 16):
        rows.append(
            push(
                ids_ref.at[z, core, x, y],
                ids_ref.at[z, core, x, y],
                xy_sem.at[0, k - 1],
                xy_sem.at[1, k - 1],
                flat[k - 1],
            )
        )
    pieces = []

    def hand(h):
        for k in range(1, 8):
            pieces.append(
                push(
                    enc_ref.at[:, piece((me + k) % 8), pl.ds(*OUT[h])],
                    pool_refs[h].at[me],
                    team_sem.at[0, h, k - 1],
                    team_sem.at[1, h, k - 1],
                    team[k - 1],
                )
            )

    hand(0)
    for copy in rows:
        copy.wait_recv()
    planes = []
    for k in range(1, 16):
        planes.append(
            push(
                ids_ref.at[z, core],
                ids_ref.at[z, core],
                zc_sem.at[0, k - 1],
                zc_sem.at[1, k - 1],
                upright[k - 1],
            )
        )
    for h in range(1, EARLY):
        hand(h)
    for copy in owns:
        copy.wait()
    for copy in planes + pieces:
        copy.wait_recv()
    for yy in range(4):
        for half in range(2):
            line = jnp.zeros((1, 128), jnp.int32)
            for zz in range(half * 4, half * 4 + 4):
                for cc in range(2):
                    for xx in range(4):
                        line = line + ids_ref[zz, cc, xx, yy]
            packed_ref[yy, half : half + 1, :] = line
    for copy in rows + pieces + planes:
        copy.wait_send()


def spread(mine, enc):
    return pl.pallas_call(
        spread_kernel,
        in_specs=[
            pl.BlockSpec(memory_space=pltpu.SMEM),
            pl.BlockSpec(memory_space=pl.ANY),
        ],
        out_specs=[pl.BlockSpec(memory_space=pltpu.VMEM)] * (EARLY + 1),
        out_shape=[jax.ShapeDtypeStruct((8, 8, 16, wide), BF) for _, wide in OUT[:EARLY]]
        + [jax.ShapeDtypeStruct((4, 2, 128), jnp.int32)],
        scratch_shapes=[
            pltpu.VMEM((8, 2, 4, 4, 1, 128), jnp.int32),
            pltpu.SemaphoreType.DMA((2, EARLY, 7)),
            pltpu.SemaphoreType.DMA((2, 15)),
            pltpu.SemaphoreType.DMA((2, 15)),
            pltpu.SemaphoreType.DMA((EARLY,)),
        ],
        compiler_params=pltpu.CompilerParams(
            collective_id=1, has_side_effects=True, vmem_limit_bytes=60 * 2**20
        ),
    )(mine, enc)


def starts(caps):
    return [0] + [sum(caps[: r + 1]) for r in range(len(caps))]


def chunks(marks, cap):
    ends = [mark for mark in marks if mark <= cap]
    return list(zip([0] + ends[:-1], ends))


def gather_kernel(caps, order_ref, loc_ref, *rest):
    count = len(OUT)
    late = count - EARLY
    enc_ref, states_ref = rest[EARLY : EARLY + 2]
    pools = rest[:EARLY] + rest[EARLY + 2 : EARLY + 2 + late]
    scratch = rest[EARLY + 2 + late :]
    packeds, arrs, stages = (scratch[k * count : k * count + count] for k in range(3))
    ring_sem, team_sem, spread_sem, own_sem = scratch[3 * count :]
    z, x, y, core = place()
    me = x * 2 + core
    total = sum(caps)
    first = starts(caps)
    marks = sorted(set(caps))
    friends = [teammate(z, y, (me + k) % 8) for k in range(1, 8)]
    ahead = at(z + 1, x, y, core)
    behind = at(z - 1, x, y, core)
    owns = []
    for h in range(EARLY, count):
        owns.append(
            pltpu.make_async_copy(
                enc_ref.at[:, piece(me), pl.ds(*OUT[h])], pools[h].at[me], own_sem.at[h - EARLY]
            )
        )
        owns[-1].start()
    greet(friends + [ahead, behind])
    copies = {}

    def forward(h, d, r, i, src, low, high):
        copies[h, d, r, i] = push(
            src,
            arrs[h].at[pl.ds(d * total + first[r] + low, high - low)],
            ring_sem.at[0, h, d, r, i],
            ring_sem.at[1, h, d, r, i],
            ahead if d == 0 else behind,
        )

    def first_hop(h):
        pool = pools[h]
        for i, (low, high) in enumerate(chunks(marks, caps[0])):
            for d in range(2):

                def fill(j, carry, d=d):
                    block = order_ref[d, j]
                    packeds[h][d, j] = pool[block // 8, block % 8]
                    return carry

                lax.fori_loop(low, high, fill, 0, unroll=2)
                forward(h, d, 0, i, packeds[h].at[d, pl.ds(low, high - low)], low, high)

        def keep(j, carry):
            for k in range(8):
                arrs[h][2 * total + j * 8 + k] = pool[j, k]
            return carry

        lax.fori_loop(0, 8, keep, 0)

    def next_hop(h, r):
        for i, (low, high) in enumerate(chunks(marks, caps[r])):
            for d in range(2):
                copies[h, d, r - 1, i].wait_recv()
                src = arrs[h].at[pl.ds(d * total + first[r - 1] + low, high - low)]
                forward(h, d, r, i, src, low, high)

    hands = []

    def hand_out(h):
        for r in range(4):
            done = len(chunks(marks, caps[r + 1])) if r < 3 else 0
            for i in range(done, len(chunks(marks, caps[r]))):
                for d in range(2):
                    copies[h, d, r, i].wait_recv()

        def pick(i, carry):
            for k in range(4):
                stages[h][i, k] = arrs[h][loc_ref[i * 4 + k]]
            return carry

        lax.fori_loop(0, 8, pick, 0)
        for k in range(1, 8):
            hands.append(
                push(
                    stages[h].at[(me + k) % 8],
                    states_ref.at[:, piece(me), pl.ds(*OUT[h])],
                    team_sem.at[0, h, k - 1],
                    team_sem.at[1, h, k - 1],
                    friends[k - 1],
                )
            )
        low, wide = OUT[h]
        states_ref[:, piece(me), low : low + wide] = stages[h][me]

    pieces = {}

    def more(h):
        for k in range(1, 8):
            pieces[h, k] = push(
                enc_ref.at[:, piece((me + k) % 8), pl.ds(*OUT[h])],
                pools[h].at[me],
                spread_sem.at[0, h - EARLY, k - 1],
                spread_sem.at[1, h - EARLY, k - 1],
                friends[k - 1],
            )

    def here(h):
        if h < EARLY:
            return
        owns[h - EARLY].wait()
        for k in range(1, 8):
            pieces[h, k].wait_recv()

    for h in range(EARLY, count):
        more(h)
    first_hop(0)
    here(1)
    first_hop(1)
    next_hop(0, 1)
    here(2)
    first_hop(2)
    next_hop(1, 1)
    next_hop(0, 2)
    next_hop(2, 1)
    next_hop(1, 2)
    next_hop(0, 3)
    next_hop(2, 2)
    next_hop(1, 3)
    hand_out(0)
    next_hop(2, 3)
    hand_out(1)
    hand_out(2)
    for copy in hands:
        copy.wait_recv()
    for copy in hands + list(pieces.values()) + list(copies.values()):
        copy.wait_send()


def gather(caps, number, order, loc, pools, enc):
    total = sum(caps)
    count = len(OUT)
    return pl.pallas_call(
        functools.partial(gather_kernel, caps),
        in_specs=[pl.BlockSpec(memory_space=pltpu.SMEM)] * 2
        + [pl.BlockSpec(memory_space=pltpu.VMEM)] * EARLY
        + [pl.BlockSpec(memory_space=pl.ANY)],
        out_specs=pl.BlockSpec(memory_space=pltpu.VMEM),
        out_shape=jax.ShapeDtypeStruct((4, 128, 512), BF),
        scratch_shapes=[pltpu.VMEM((8, 8, 16, wide), BF) for _, wide in OUT[EARLY:]]
        + [pltpu.VMEM((2, caps[0], 16, wide), BF) for _, wide in OUT]
        + [pltpu.VMEM((2 * total + 64, 16, wide), BF) for _, wide in OUT]
        + [pltpu.VMEM((8, 4, 16, wide), BF) for _, wide in OUT]
        + [
            pltpu.SemaphoreType.DMA((2, count, 2, 4, 4)),
            pltpu.SemaphoreType.DMA((2, count, 7)),
            pltpu.SemaphoreType.DMA((2, count - EARLY, 7)),
            pltpu.SemaphoreType.DMA((count - EARLY,)),
        ],
        compiler_params=pltpu.CompilerParams(
            collective_id=number, has_side_effects=True, vmem_limit_bytes=60 * 2**20
        ),
    )(order, loc, *pools, enc)


def finish_kernel(
    caps,
    mate_ref,
    con_ref,
    fin_ref,
    ge_ref,
    sums_ref,
    gs_ref,
    gw_ref,
    *scratch,
):
    count = len(BACK)
    takens, combs, outbs, inbs, dones = (scratch[k * count : k * count + count] for k in range(5))
    held, y_in, x_half, x_in, z_in, team_sem, ring_sem, home_sem, y_sem, x_sem, z_sem = scratch[
        5 * count :
    ]
    z, x, y, core = place()
    me = x * 2 + core
    total = sum(caps)
    first = starts(caps)
    marks = sorted(set(caps))
    friends = [teammate(z, y, (me + k) % 8) for k in range(1, 8)]
    around = [at(z + k, x, y, core) for k in range(1, 8)]
    ahead = around[0]
    behind = around[6]
    sides = [at(z, x, y + 1, core), at(z, x, y - 1, core)]
    greet(friends + around + sides)

    def send(src, dst, sems, slot, target):
        return push(src, dst, sems.at[0, slot], sems.at[1, slot], target)

    given = []

    def give(h):
        for k in range(1, 8):
            given.append(
                push(
                    ge_ref.at[:, piece((me + k) % 8), pl.ds(*BACK[h])],
                    takens[h].at[pl.ds(me * 4, 4)],
                    team_sem.at[0, h, k - 1],
                    team_sem.at[1, h, k - 1],
                    friends[k - 1],
                )
            )

    give(0)
    up = send(sums_ref.at[0], y_in.at[0], y_sem, 0, sides[0])
    down = send(sums_ref.at[2], y_in.at[1], y_sem, 1, sides[1])
    give(1)
    give(2)

    def combine(h):
        taken, comb = takens[h], combs[h]
        low, wide = BACK[h]
        taken[pl.ds(me * 4, 4)] = ge_ref[:, piece(me), low : low + wide]
        taken[32] = jnp.zeros((16, wide), BF)
        comb[32] = jnp.zeros((16, wide), F32)
        inbs[h][2 * total] = jnp.zeros((16, wide), BF)
        for copy in given[h * 7 : h * 7 + 7]:
            copy.wait_recv()

        def step(i, carry):
            row = taken[mate_ref[0, i]].astype(F32)
            for t in range(1, 4):
                row = row + taken[mate_ref[t, i]].astype(F32)
            comb[i] = row
            return carry

        lax.fori_loop(0, 32, step, 0, unroll=4)

    copies = {}

    def back(h, r, i, added):
        comb, inb, outb = combs[h], inbs[h], outbs[h]
        low, high = chunks(marks, caps[r])[i]
        for d in range(2):
            base = d * total + first[r]
            if added:
                copies[h, d, r + 1, i].wait_recv()
                further = d * total + first[r + 1]

                def fill(j, carry, d=d, base=base, further=further):
                    outb[base + j] = (
                        comb[con_ref[d, r, j]] + inb[further + j].astype(F32)
                    ).astype(BF)
                    return carry
            else:

                def fill(j, carry, d=d, base=base):
                    outb[base + j] = comb[con_ref[d, r, j]].astype(BF)
                    return carry

            lax.fori_loop(low, high, fill, 0, unroll=2)
            copies[h, d, r, i] = push(
                outb.at[pl.ds(base + low, high - low)],
                inb.at[pl.ds(base + low, high - low)],
                ring_sem.at[0, h, d, r, i],
                ring_sem.at[1, h, d, r, i],
                behind if d == 0 else ahead,
            )

    def farthest(h):
        for i in range(len(chunks(marks, caps[3]))):
            back(h, 3, i, False)
        for r in (2, 1, 0):
            for i in range(len(chunks(marks, caps[r + 1])), len(chunks(marks, caps[r]))):
                back(h, r, i, False)

    def nearer(h, r):
        for i in range(len(chunks(marks, caps[r + 1]))):
            back(h, r, i, True)

    homes = []

    def go_home(h):
        comb, inb = combs[h], inbs[h]
        for i in range(len(chunks(marks, caps[0]))):
            for d in range(2):
                copies[h, d, 0, i].wait_recv()

        def close(i, carry):
            for k in range(8):
                b = i * 8 + k
                dones[h][i, k] = (
                    inb[fin_ref[0, b]].astype(F32)
                    + inb[fin_ref[1, b]].astype(F32)
                    + comb[fin_ref[2, b]]
                ).astype(BF)
            return carry

        lax.fori_loop(0, 8, close, 0)
        for k in range(1, 8):
            homes.append(
                push(
                    dones[h].at[(me + k) % 8],
                    gs_ref.at[:, piece(me), pl.ds(*BACK[h])],
                    home_sem.at[0, h, k - 1],
                    home_sem.at[1, h, k - 1],
                    friends[k - 1],
                )
            )
        low, wide = BACK[h]
        gs_ref[:, piece(me), low : low + wide] = dones[h][me]

    def y_total(offset):
        part = (x + offset) % 4
        return (
            sums_ref[1, part].astype(F32)
            + y_in[0, part].astype(F32)
            + y_in[1, part].astype(F32)
        )

    combine(0)
    farthest(0)
    combine(1)
    nearer(0, 2)
    farthest(1)
    nearer(0, 1)
    combine(2)
    nearer(1, 2)
    nearer(0, 0)
    farthest(2)
    left = at(z, x - 1, y, core)
    right = at(z, x + 1, y, core)
    up.wait_recv()
    down.wait_recv()
    held[0] = y_total(2).astype(BF)
    xup = send(held.at[0, 0], x_half.at[0], x_sem, 0, right)
    xdown = send(held.at[0, 1], x_half.at[1], x_sem, 1, left)
    nearer(1, 1)
    ahead_x = y_total(1)
    xup.wait_recv()
    held[1, 0] = (ahead_x[0] + x_half[0].astype(F32)).astype(BF)
    held[1, 1] = ahead_x[1].astype(BF)
    xup2 = send(held.at[1], x_in.at[0], x_sem, 2, right)
    behind_x = y_total(3)
    xdown.wait_recv()
    held[2, 0] = behind_x[0].astype(BF)
    held[2, 1] = (behind_x[1] + x_half[1].astype(F32)).astype(BF)
    xdown2 = send(held.at[2], x_in.at[1], x_sem, 3, left)
    go_home(0)
    nearer(2, 2)
    nearer(1, 0)
    xup2.wait_recv()
    xdown2.wait_recv()
    held[3] = (y_total(0) + x_in[0].astype(F32) + x_in[1].astype(F32)).astype(BF)
    zs = []
    for step in (4, 3, 5, 2, 6, 1, 7):
        target = (z + step) % 8
        zs.append(
            send(held.at[3, :, target], z_in.at[step - 1], z_sem, step - 1, around[step - 1])
        )
    nearer(2, 1)
    go_home(1)
    nearer(2, 0)
    go_home(2)
    result = held[3, :, z].astype(F32)
    for copy, step in zip(zs, (4, 3, 5, 2, 6, 1, 7)):
        copy.wait_recv()
        result = result + z_in[step - 1].astype(F32)
    gw_ref[...] = result
    for copy in homes:
        copy.wait_recv()
    rest = [up, down, xup, xdown, xup2, xdown2] + zs
    for copy in given + homes + rest + list(copies.values()):
        copy.wait_send()


def finish(caps, number, mate, con, fin, ge, sums):
    total = sum(caps)
    count = len(BACK)
    smem = pl.BlockSpec(memory_space=pltpu.SMEM)
    vmem = pl.BlockSpec(memory_space=pltpu.VMEM)
    return pl.pallas_call(
        functools.partial(finish_kernel, caps),
        in_specs=[smem, smem, smem, vmem, vmem],
        out_specs=[vmem, vmem],
        out_shape=[
            jax.ShapeDtypeStruct((8, 128, 512), BF),
            jax.ShapeDtypeStruct((2, 16, 256), F32),
        ],
        scratch_shapes=[pltpu.VMEM((33, 16, wide), BF) for _, wide in BACK]
        + [pltpu.VMEM((33, 16, wide), F32) for _, wide in BACK]
        + [pltpu.VMEM((2 * total, 16, wide), BF) for _, wide in BACK]
        + [pltpu.VMEM((2 * total + 1, 16, wide), BF) for _, wide in BACK]
        + [pltpu.VMEM((8, 8, 16, wide), BF) for _, wide in BACK]
        + [
            pltpu.VMEM((4, 2, 8, 16, 256), BF),
            pltpu.VMEM((2, 4, 2, 8, 16, 256), BF),
            pltpu.VMEM((2, 8, 16, 256), BF),
            pltpu.VMEM((2, 2, 8, 16, 256), BF),
            pltpu.VMEM((7, 2, 16, 256), BF),
            pltpu.SemaphoreType.DMA((2, count, 7)),
            pltpu.SemaphoreType.DMA((2, count, 2, 4, 4)),
            pltpu.SemaphoreType.DMA((2, count, 7)),
            pltpu.SemaphoreType.DMA((2, 2)),
            pltpu.SemaphoreType.DMA((2, 4)),
            pltpu.SemaphoreType.DMA((2, 7)),
        ],
        compiler_params=pltpu.CompilerParams(
            collective_id=number, has_side_effects=True, vmem_limit_bytes=48 * 2**20
        ),
    )(mate, con, fin, ge, sums)


TIGHT = (22, 18, 14, 6)
MIDDLE = (24, 20, 16, 8)
WIDE = (64, 64, 64, 32)
CAPS = (TIGHT, MIDDLE, WIDE)


def plan(ids):
    z, x, y, core = place()
    i32 = jnp.int32
    place_of = jnp.arange(256, dtype=i32)[None, :]
    block = (ids // 8 % 4 * 2 + place_of // 4 % 2) * 8 + ids % 8
    owner_z = ids // 32
    away = (place_of // 32 - owner_z + 8) % 8
    flat = owner_z * 64 + block
    is_block = (flat[:, None, :] == jnp.arange(512, dtype=i32)[None, :, None]).astype(BF)
    is_away = (away[:, None, :] == jnp.arange(8, dtype=i32)[None, :, None]).astype(BF)
    wanted = jnp.einsum("ydr,ybr->ydb", is_away, is_block, preferred_element_type=F32) > 0.5
    wanted = wanted.reshape(4, 8, 8, 64)
    team = jnp.arange(64, dtype=i32)
    even = team % 2 == 0

    def far(one, two, three, four):
        return jnp.where(four, 4, jnp.where(three, 3, jnp.where(two, 2, jnp.where(one, 1, 0))))

    up = far(wanted[:, 1], wanted[:, 2], wanted[:, 3], wanted[:, 4] & even)
    down = far(wanted[:, 7], wanted[:, 6], wanted[:, 5], wanted[:, 4] & ~even)
    fars = jnp.stack([up, down], axis=1).astype(i32)
    reach = jnp.arange(1, 5, dtype=i32)[:, None, None, None, None]
    lengths = jnp.sum((fars[None] >= reach).astype(i32), axis=-1)
    longest = jnp.max(lengths, axis=(1, 2, 3))
    level = jnp.where(
        jnp.all(longest <= jnp.array(TIGHT, i32)),
        0,
        jnp.where(jnp.all(longest <= jnp.array(MIDDLE, i32)), 1, 2),
    )
    fars = lax.dynamic_index_in_dim(fars, y, 0, keepdims=False)
    fars = lax.dynamic_slice_in_dim(jnp.concatenate([fars, fars], axis=1), z, 8, axis=1)
    key = fars * 64 + 63 - team
    rank = jnp.sum((key[..., :, None] > key[..., None, :]).astype(i32), axis=-2)
    at_rank = rank[..., :, None] == team
    order = jnp.sum(jnp.where(at_rank[:, 0], team[:, None], 0), axis=-2)

    def mine(a):
        return lax.dynamic_slice(a, (y, z * 32), (1, 32)).reshape(32)

    my_block, my_away = mine(block), mine(away)
    my_flat = (8 - my_away) % 8 * 64 + my_block
    upwards = (my_away < 4) | ((my_away == 4) & (my_block % 2 == 0))
    hops = jnp.where(upwards, my_away, 8 - my_away)
    hit = my_flat[:, None] == jnp.arange(512, dtype=i32)[None, :]
    ranks = lax.dot_general(
        rank.reshape(2, 512).astype(BF), hit.astype(BF), NT, preferred_element_type=F32
    ).astype(i32)
    spot = jnp.where(upwards, ranks[0], ranks[1])
    refs = jnp.arange(32, dtype=i32)
    first = jnp.min(jnp.where(hit, refs[:, None], 32), axis=0).reshape(8, 64)
    same = my_flat[:, None] == my_flat[None, :]
    earlier = jnp.sum(
        (same[None] & (refs[None, :, None] < refs[:, None, None])).astype(i32), axis=1
    )
    turns = jnp.arange(4, dtype=i32)[:, None, None]
    mate = 32 + jnp.sum(
        jnp.where(same[None] & (earlier[None] == turns), refs[:, None] - 32, 0), axis=1
    )
    firsts = jnp.stack(
        [
            jnp.stack([first[7], first[6], first[5], jnp.where(even, first[4], 32)]),
            jnp.stack([first[1], first[2], first[3], jnp.where(even, 32, first[4])]),
        ]
    )
    at_rank_by_hop = jnp.stack(
        [
            jnp.stack([at_rank[0, 7], at_rank[0, 6], at_rank[0, 5], at_rank[0, 4]]),
            jnp.stack([at_rank[1, 1], at_rank[1, 2], at_rank[1, 3], at_rank[1, 4]]),
        ]
    )
    con = 32 + jnp.sum(jnp.where(at_rank_by_hop, firsts[..., None] - 32, 0), axis=-2)

    def locate(caps):
        total = sum(caps)
        offset = sum(jnp.where(hops == r + 1, starts(caps)[r], 0) for r in range(4))
        there = jnp.where(upwards, 0, total) + offset + spot
        return jnp.where(my_away == 0, 2 * total + my_block, there)

    def collect(caps):
        total = sum(caps)
        return jnp.stack(
            [
                jnp.where(fars[0, 0] > 0, rank[0, 0], 2 * total),
                jnp.where(fars[1, 0] > 0, total + rank[1, 0], 2 * total),
                first[0],
            ]
        )

    return level, order, mate, con, locate, collect


def body(queries, grad_out, enc_states, neighbour_ids, kv_weight):
    enc = enc_states[0]
    *pools, ids = spread(neighbour_ids, enc)
    level, order, mate, con, locate, collect = plan(ids.reshape(4, 256))
    states = lax.switch(
        level,
        [
            lambda caps=caps, number=number: gather(caps, number, order, locate(caps), pools, enc)
            for caps, number in zip(CAPS, (2, 3, 7))
        ],
    )
    gq, grad_e, sums = attention(states.reshape(512, 512), kv_weight, queries[0], grad_out[0])
    grad_e = grad_e.reshape(4, 128, 512)
    grad_states, grad_weight = lax.switch(
        level,
        [
            lambda caps=caps, number=number: finish(
                caps, number, mate, con, collect(caps), grad_e, sums
            )
            for caps, number in zip(CAPS, (4, 5, 8))
        ],
    )
    return (gq[None], grad_states[None], grad_weight)


def solution(mesh):
    placed = (
        P("grp", "seq", None),
        P("grp", "seq", None),
        P("grp", "seq", None, None),
        P("grp", "seq", None),
        P(),
    )
    return jax.shard_map(
        body,
        mesh=mesh,
        in_specs=placed,
        out_specs=(P("grp", "seq", None), P("grp", "seq", None, None), P(None, "seq", "grp")),
        check_vma=False,
    )
```
